768 devices in a mesh: leaf: 64 (over y, x, core), grp: 12 (over z).
Axes of the slice: x: 4, y: 8, z: 12, core: 2. Of those that a mesh axis runs over, the one named last changes fastest.
Arguments:
- moments: bfloat16 [786432, 256], P(('leaf', 'grp')), may hold values from -6 to 6
- live_fine: int32 [768], P(('leaf', 'grp')), may hold values from 64 to 1024, as said below
- near_requests: int32 [9216, 32], P(('leaf', 'grp')), may hold values from 0 to 1151, as said below
- far_requests: int32 [49152, 8], P(('leaf', 'grp')), may hold values from 1024 to 1167, as said below
- pair_source: int32 [12288, 1168], P(('leaf', 'grp')), may hold values from 0 to 2064, as said below
- child_up: bfloat16 [8, 256, 256], replicated, may hold values from -0.125 to 0.125
- child_down: bfloat16 [8, 256, 256], replicated, may hold values from -0.375 to 0.375
- offset_ops: bfloat16 [16, 256, 256], replicated, may hold values from -0.09375 to 0.09375
Outputs:
- expansions: bfloat16 [786432, 256], P(('leaf', 'grp'))
The draws below stay inside these ranges and needn't reach their ends.
Inputs may be any that keep to these rules, and one draw needn't show every extreme that they name: `live_fine`: live cells of a device come first in its range; its middle and coarsest levels have ceil(n / 8) and ceil(n / 64) live cells. Some device has all 1024 live, some only 64. `near_requests`: A device's row g names, as indices into the cells of the device at position g of its group, 24 live finest-level cells and then 8 live middle-level cells. `far_requests`: A device's row l names, as indices into the cells of the device with leaf index l and the same grp index, 6 live middle-level cells and then 2 live coarsest cells. `pair_source`: A source row holds a cell of the target's level; cells that are not live take no source. Coarsest cells take sources from the leaf requests only.
All inputs are finite; a program needn't handle non-finite values.
Results may differ from the reference program's by a relative error of at most 0.01.
Values may be sent and summed in bfloat16 or wider, within the bound.
No kernel may reach another device: no remote copies, remote signals or barrier semaphores. Data moves between devices by JAX's collectives and lax.ppermute only.
A program may use at most 32 MiB of HBM per device.

```python
import jax
import jax.numpy as jnp
from jax import lax

P_SIZE = 256
OFFSETS = 16
F = 1024
RGF = 24
RGM = 8
RLM = 6
RLC = 2
RG = 32
RL = 8
CELLS = 1168
TABLE = 2064
N_LEAF = 64
N_GRP = 12
DEVICES = 768


def live_counts(key):
    key = jax.random.fold_in(key, 7)
    subkeys = jax.random.split(key, 3)
    baseline = F // 16 + jax.random.randint(subkeys[0], (DEVICES,), 0, F * 7 // 16 + 1)
    crowded = jax.random.randint(subkeys[1], (DEVICES,), 0, 16) == 0
    counts = jnp.where(crowded, F, baseline)
    fullest = jax.random.randint(subkeys[2], (), 0, DEVICES)
    counts = counts.at[fullest].set(F)
    counts = counts.at[(fullest + 1) % DEVICES].set(F // 16)
    return (counts.astype(jnp.int32), fullest)


def draw_live_fine(key, part):
    counts, fullest = live_counts(key)
    return counts


def draw_near_requests(key, part):
    counts, fullest = live_counts(key)
    key = jax.random.fold_in(key, 11)
    device = jnp.arange(DEVICES, dtype=jnp.int32)[:, None]
    position = jnp.arange(N_GRP, dtype=jnp.int32)[None, :]
    neighbour = device // N_GRP * N_GRP + position
    peer_fine = counts[neighbour][:, :, None]
    peer_middle = (peer_fine + 7) // 8
    slot_index = jnp.arange(RG, dtype=jnp.int32)[None, None, :]
    random_bits = jax.random.randint(key, (DEVICES, N_GRP, RG), 0, 1 << 30)
    cell_ids = jnp.where(slot_index < RGF, random_bits % peer_fine, F + random_bits % peer_middle)
    own_pos = fullest % N_GRP
    cell_ids = cell_ids.at[fullest, own_pos, RG - 1].set(F + F // 8 - 1)
    cell_ids = cell_ids.at[fullest, own_pos, 0].set(0)
    return cell_ids.reshape(DEVICES * N_GRP, RG).astype(jnp.int32)


def draw_far_requests(key, part):
    counts, fullest = live_counts(key)
    key = jax.random.fold_in(key, 12)
    device = jnp.arange(DEVICES, dtype=jnp.int32)[:, None]
    position = jnp.arange(N_LEAF, dtype=jnp.int32)[None, :]
    neighbour = position * N_GRP + device % N_GRP
    peer_fine = counts[neighbour][:, :, None]
    peer_middle = (peer_fine + 7) // 8
    peer_coarse = (peer_fine + 63) // 64
    slot_index = jnp.arange(RL, dtype=jnp.int32)[None, None, :]
    random_bits = jax.random.randint(key, (DEVICES, N_LEAF, RL), 0, 1 << 30)
    cell_ids = jnp.where(slot_index < RLM, F + random_bits % peer_middle, F + F // 8 + random_bits % peer_coarse)
    own_pos = fullest // N_GRP
    cell_ids = cell_ids.at[fullest, own_pos, RL - 1].set(CELLS - 1)
    cell_ids = cell_ids.at[fullest, own_pos, 0].set(F)
    return cell_ids.reshape(DEVICES * N_LEAF, RL).astype(jnp.int32)


def draw_pair_source(key, part):
    counts, fullest = live_counts(key)
    key = jax.random.fold_in(key, 13)
    subkeys = jax.random.split(key, 2)
    random_bits = jax.random.randint(subkeys[0], (DEVICES, OFFSETS, CELLS), 0, 1 << 30)
    missing = jax.random.randint(subkeys[1], (DEVICES, OFFSETS, CELLS), 0, 10) < 3
    cell_index = jnp.arange(CELLS, dtype=jnp.int32)[None, None, :]
    fine_live = counts[:, None, None]
    middle_live = (fine_live + 7) // 8
    coarse_live = (fine_live + 63) // 64
    near_base = CELLS
    far_base = CELLS + N_GRP * RG
    picked = random_bits % (fine_live + N_GRP * RGF)
    offset_near = picked - fine_live
    fine_source = jnp.where(picked < fine_live, picked, near_base + offset_near // RGF * RG + offset_near % RGF)
    picked = random_bits % (middle_live + N_GRP * RGM + N_LEAF * RLM)
    offset_near = picked - middle_live
    offset_far = offset_near - N_GRP * RGM
    middle_source = jnp.where(picked < middle_live, F + picked, jnp.where(offset_near < N_GRP * RGM, near_base + offset_near // RGM * RG + RGF + offset_near % RGM, far_base + offset_far // RLM * RL + offset_far % RLM))
    picked = random_bits % (N_LEAF * RLC)
    coarse_source = far_base + picked // RLC * RL + RLM + picked % RLC
    is_fine = cell_index < F
    is_middle = cell_index < F + F // 8
    level_index = cell_index - jnp.where(is_fine, 0, jnp.where(is_middle, F, F + F // 8))
    alive = level_index < jnp.where(is_fine, fine_live, jnp.where(is_middle, middle_live, coarse_live))
    source = jnp.where(is_fine, fine_source, jnp.where(is_middle, middle_source, coarse_source))
    source = jnp.where(alive & jnp.logical_not(missing), source, TABLE)
    return source.reshape(DEVICES * OFFSETS, CELLS).astype(jnp.int32)


def block_levels(key, shape, shards, least, high):
    gain, own = 1.0, jax.random.fold_in(key, 6)
    for dim, blocks in shards:
        heights = jnp.exp(jax.random.uniform(jax.random.fold_in(own, dim), (blocks,), jnp.float32, least / len(shards), high / len(shards)))
        gain = gain * jnp.repeat(heights, shape[dim] // blocks).reshape([-1 if axis == dim else 1 for axis in range(len(shape))])
    return gain


def scatter_about(own_key, dims, scale, reach, cuts=(), kind=jnp.bfloat16):
    entries = scale * jax.random.normal(own_key, dims, jnp.float32)
    if cuts:
        entries = entries * block_levels(own_key, dims, cuts, -0.22, 0.18)
    return jnp.clip(entries, -reach, reach).astype(kind)


def setup_inputs(seed: int = 0) -> dict:
    keys = jax.random.split(jax.random.key(seed), 9)
    moments = scatter_about(keys[0], (DEVICES * F, P_SIZE), 1.0, 6.0, ((0, 768),))
    live_fine = draw_live_fine(jax.random.fold_in(keys[8], 71), 0)
    near_requests = draw_near_requests(jax.random.fold_in(keys[8], 71), 0)
    far_requests = draw_far_requests(jax.random.fold_in(keys[8], 71), 0)
    pair_source = draw_pair_source(jax.random.fold_in(keys[8], 71), 0)
    child_up = scatter_about(keys[5], (8, P_SIZE, P_SIZE), (8 * P_SIZE) ** -0.5, 0.125)
    child_down = scatter_about(keys[6], (8, P_SIZE, P_SIZE), P_SIZE ** -0.5, 0.375)
    offset_ops = scatter_about(keys[7], (OFFSETS, P_SIZE, P_SIZE), (P_SIZE * OFFSETS) ** -0.5, 0.09375)
    return dict(moments=moments, live_fine=live_fine, near_requests=near_requests, far_requests=far_requests, pair_source=pair_source, child_up=child_up, child_down=child_down, offset_ops=offset_ops)


def upward_pass(block, child_up):
    upward = child_up.reshape(8 * P_SIZE, P_SIZE)
    middle = jnp.dot(block.reshape(F // 8, 8 * P_SIZE), upward, preferred_element_type=jnp.float32).astype(jnp.bfloat16)
    coarse = jnp.dot(middle.reshape(F // 64, 8 * P_SIZE), upward, preferred_element_type=jnp.float32).astype(jnp.bfloat16)
    return jnp.concatenate([block, middle, coarse], axis=0)


def downward(parents, child_down):
    spread = jnp.einsum("cp,kpq->ckq", parents.astype(jnp.float32), child_down.astype(jnp.float32))
    return spread.reshape(parents.shape[0] * 8, P_SIZE)


def reference(moments, live_fine, near_requests, far_requests, pair_source, child_up, child_down, offset_ops):
    blocks = moments.reshape(DEVICES, F, P_SIZE)
    alive = jnp.arange(F, dtype=jnp.int32)[None, :] < live_fine[:, None]
    blocks = jnp.where(alive[:, :, None], blocks, jnp.zeros((), blocks.dtype))
    all_cells = lax.map(lambda block: upward_pass(block, child_up), blocks)
    near_all = near_requests.reshape(DEVICES, N_GRP, RG)
    far_all = far_requests.reshape(DEVICES, N_LEAF, RL)
    pairs_all = pair_source.reshape(DEVICES, OFFSETS, CELLS)
    operators = offset_ops.reshape(OFFSETS * P_SIZE, P_SIZE)

    def per_device(inputs):
        device, near_rows, far_rows, pairs, alive_row = inputs
        near_peer = (device // N_GRP) * N_GRP + jnp.arange(N_GRP, dtype=jnp.int32)
        far_peer = jnp.arange(N_LEAF, dtype=jnp.int32) * N_GRP + device % N_GRP
        near_tiles = all_cells[near_peer[:, None], near_rows]
        far_tiles = all_cells[far_peer[:, None], far_rows]
        sources = jnp.concatenate([all_cells[device], near_tiles.reshape(N_GRP * RG, P_SIZE), far_tiles.reshape(N_LEAF * RL, P_SIZE)], axis=0)
        picked = jnp.take(sources, pairs.T, axis=0, mode="fill", fill_value=0)
        far_field = jnp.dot(picked.reshape(CELLS, OFFSETS * P_SIZE), operators, preferred_element_type=jnp.float32)
        coarse_local = far_field[F + F // 8:].astype(jnp.bfloat16)
        middle_local = (far_field[F:F + F // 8] + downward(coarse_local, child_down)).astype(jnp.bfloat16)
        expansion = far_field[:F] + downward(middle_local, child_down)
        return jnp.where(alive_row[:, None], expansion, jnp.zeros((), expansion.dtype)).astype(jnp.bfloat16)

    device_ids = jnp.arange(DEVICES, dtype=jnp.int32)
    result = lax.map(per_device, (device_ids, near_all, far_all, pairs_all, alive))
    return result.reshape(DEVICES * F, P_SIZE)
```

```python
import functools

import jax
import jax.numpy as jnp
from jax import lax
from jax.experimental import pallas as pl
from jax.experimental.pallas import tpu as pltpu
from jax.sharding import PartitionSpec as P

BF16 = jnp.bfloat16
F32 = jnp.float32
TILE = 256
VMEM = pl.BlockSpec(memory_space=pltpu.VMEM)


def one_hot(column, base, width):
    rows = column.shape[0]
    wide = jnp.broadcast_to(column - base, (rows, 128)).astype(jnp.int16)
    lane = lax.broadcasted_iota(jnp.int32, (rows, 128), 1).astype(jnp.int16)
    one = jnp.ones((rows, 128), BF16)
    zero = jnp.zeros((rows, 128), BF16)
    parts = [jnp.where(wide == lane + jnp.int16(128 * k), one, zero) for k in range(width // 128)]
    return parts[0] if len(parts) == 1 else jnp.concatenate(parts, axis=1)


def dot(a, b):
    return jnp.dot(a, b, preferred_element_type=F32)


def own_kernel(first, offsets, fine_ref, pairs_ref, ops_ref, *refs):
    if first:
        out_ref, moved_ref = refs
    else:
        in_ref, out_ref, moved_ref = refs
    count = fine_ref.shape[0]
    for n, o in enumerate(offsets):
        moved_ref[n % 2] = dot(fine_ref[...], ops_ref[o]).astype(BF16)
        for m in range(count // TILE):
            rows = slice(m * TILE, (m + 1) * TILE)
            part = dot(one_hot(pairs_ref[rows, o : o + 1], 0, count), moved_ref[n % 2])
            if n > 0:
                part = part + out_ref[rows, :]
            elif not first:
                part = part + in_ref[rows, :]
            out_ref[rows, :] = part


def own_pass(fine, pairs, ops, offsets, total):
    count, size = fine.shape
    first = total is None
    args = (fine, pairs, ops) if first else (fine, pairs, ops, total)
    macs = len(offsets) * count * size * (size + count)
    return pl.pallas_call(
        functools.partial(own_kernel, first, offsets),
        out_shape=jax.ShapeDtypeStruct((count, size), F32),
        in_specs=[VMEM] * len(args),
        out_specs=VMEM,
        scratch_shapes=[pltpu.VMEM((2, count, size), BF16)],
        compiler_params=pltpu.CompilerParams(vmem_limit_bytes=24 << 20),
        cost_estimate=pl.CostEstimate(flops=2 * macs, bytes_accessed=4 << 20, transcendentals=0),
        name="own_pass",
    )(*args)


def near_kernel(near_base, near_ref, mid_ref, pairs_ref, ops_ref, total_ref, out_ref, out_mid_ref, moved_ref, picked_ref):
    count = total_ref.shape[0]
    middles = mid_ref.shape[0]
    near = near_ref.shape[0]
    offsets = ops_ref.shape[0]
    for o in range(offsets):
        moved_ref[o % 2] = dot(near_ref[...], ops_ref[o]).astype(BF16)
        for m in range(count // TILE):
            rows = slice(m * TILE, (m + 1) * TILE)
            part = dot(one_hot(pairs_ref[rows, o : o + 1], near_base, near), moved_ref[o % 2])
            if o > 0:
                part = part + out_ref[rows, :]
            else:
                part = part + total_ref[rows, :]
            out_ref[rows, :] = part
    for o in range(offsets):
        column = pairs_ref[count : count + middles, o : o + 1]
        part = dot(one_hot(column, count, middles), mid_ref[...])
        part = part + dot(one_hot(column, near_base, near), near_ref[...])
        picked_ref[o] = part.astype(BF16)
    mid = dot(picked_ref[0], ops_ref[0])
    for o in range(1, offsets):
        mid = mid + dot(picked_ref[o], ops_ref[o])
    out_mid_ref[...] = mid


def near_pass(near_base, near, mid, pairs, ops, total):
    count, size = total.shape
    offsets = ops.shape[0]
    macs = offsets * near.shape[0] * size * (size + count)
    return pl.pallas_call(
        functools.partial(near_kernel, near_base),
        out_shape=(
            jax.ShapeDtypeStruct((count, size), F32),
            jax.ShapeDtypeStruct(mid.shape, F32),
        ),
        in_specs=[VMEM] * 5,
        out_specs=(VMEM, VMEM),
        scratch_shapes=[
            pltpu.VMEM((2,) + near.shape, BF16),
            pltpu.VMEM((offsets,) + mid.shape, BF16),
        ],
        compiler_params=pltpu.CompilerParams(vmem_limit_bytes=24 << 20),
        cost_estimate=pl.CostEstimate(flops=2 * macs, bytes_accessed=6 << 20, transcendentals=0),
        name="near_pass",
    )(near, mid, pairs, ops, total)


def far_kernel(far_base, live_ref, far_ref, pairs_ref, ops_ref, down_ref, mid_ref, total_ref, out_ref, picked_ref, mid_wide, fine_wide):
    count = total_ref.shape[0]
    middles = mid_ref.shape[0]
    cells = pairs_ref.shape[0]
    far = far_ref.shape[0]
    offsets = ops_ref.shape[0]
    for o in range(offsets):
        column = pairs_ref[:, o : o + 1]
        picked_ref[o] = dot(one_hot(column, far_base, far), far_ref[...]).astype(BF16)
    field = dot(picked_ref[0], ops_ref[0])
    for o in range(1, offsets):
        field = field + dot(picked_ref[o], ops_ref[o])
    coarse = field[middles:, :].astype(BF16)
    coarses = cells - middles
    for k in range(8):
        rows = pl.ds(k, coarses, stride=8)
        spread = dot(coarse, down_ref[k])
        mid_wide[0, rows, :] = spread[:, :128]
        mid_wide[1, rows, :] = spread[:, 128:]
    spread = jnp.concatenate([mid_wide[0], mid_wide[1]], axis=1)
    mid = (field[:middles, :] + mid_ref[...] + spread).astype(BF16)
    for k in range(8):
        rows = pl.ds(k, middles, stride=8)
        spread = dot(mid, down_ref[k])
        fine_wide[0, rows, :] = spread[:, :128]
        fine_wide[1, rows, :] = spread[:, 128:]
    live = live_ref[0]
    for m in range(count // TILE):
        rows = slice(m * TILE, (m + 1) * TILE)
        row = lax.broadcasted_iota(jnp.int32, (TILE, 1), 0) + m * TILE
        spread = jnp.concatenate([fine_wide[0, rows, :], fine_wide[1, rows, :]], axis=1)
        out_ref[rows, :] = jnp.where(row < live, total_ref[rows, :] + spread, 0.0).astype(BF16)


def far_pass(far_base, live, far, pairs, ops, down, mid, total):
    count, size = total.shape
    offsets = ops.shape[0]
    cells = pairs.shape[0]
    macs = offsets * cells * size * (far.shape[0] + size) + count * size * size
    return pl.pallas_call(
        functools.partial(far_kernel, far_base),
        out_shape=jax.ShapeDtypeStruct((count, size), BF16),
        in_specs=[pl.BlockSpec(memory_space=pltpu.SMEM)] + [VMEM] * 6,
        out_specs=VMEM,
        scratch_shapes=[
            pltpu.VMEM((offsets, cells, size), BF16),
            pltpu.VMEM((2, mid.shape[0], 128), F32),
            pltpu.VMEM((2, count, 128), F32),
        ],
        compiler_params=pltpu.CompilerParams(vmem_limit_bytes=24 << 20),
        cost_estimate=pl.CostEstimate(flops=2 * macs, bytes_accessed=6 << 20, transcendentals=0),
        name="far_pass",
    )(live, far, pairs, ops, down, mid, total)


def exchange(rows, axis):
    return lax.all_to_all(rows, axis, split_axis=0, concat_axis=0, tiled=True)


def pick(table, index):
    rows = jnp.take(table, index.reshape(-1), axis=0, mode="clip")
    return rows.reshape(index.shape + table.shape[1:])


def body(
    moments, live_fine, near_requests, far_requests, pair_source, child_up, child_down, offset_ops
):
    fine_count, size = moments.shape
    middle_count = fine_count // 8
    coarse_count = fine_count // 64
    cells = fine_count + middle_count + coarse_count
    offsets = offset_ops.shape[0]
    near_asked = exchange(near_requests, "grp")
    far_asked = exchange(far_requests, "leaf")
    alive = jnp.arange(fine_count, dtype=jnp.int32)[:, None] < live_fine[0]
    fine = jnp.where(alive, moments, jnp.zeros((), moments.dtype))
    upward = child_up.reshape(8 * size, size)
    middle = dot(fine.reshape(middle_count, 8 * size), upward).astype(BF16)
    coarse = dot(middle.reshape(coarse_count, 8 * size), upward).astype(BF16)
    pairs = pair_source.T
    near_tiles = exchange(pick(jnp.concatenate([fine, middle]), near_asked), "grp")
    far_tiles = exchange(pick(jnp.concatenate([middle, coarse]), far_asked - fine_count), "leaf")
    near_tiles = near_tiles.reshape(-1, size)
    far_tiles = far_tiles.reshape(-1, size)
    half = offsets // 2
    total = own_pass(fine, pairs, offset_ops, tuple(range(half)), None)
    total = own_pass(fine, pairs, offset_ops, tuple(range(half, offsets)), total)
    total, mid = near_pass(cells, near_tiles, middle, pairs, offset_ops, total)
    far_base = cells + near_tiles.shape[0]
    return far_pass(
        far_base, live_fine, far_tiles, pairs[fine_count:], offset_ops, child_down, mid, total
    )


def solution(mesh):
    in_specs = (
        P(("leaf", "grp"), None),
        P(("leaf", "grp")),
        P(("leaf", "grp"), None),
        P(("leaf", "grp"), None),
        P(("leaf", "grp"), None),
        P(),
        P(),
        P(),
    )
    out_specs = P(("leaf", "grp"), None)
    return jax.shard_map(body, mesh=mesh, in_specs=in_specs, out_specs=out_specs, check_vma=False)
```

```python
import functools

import jax
import jax.numpy as jnp
from jax import lax
from jax.experimental import pallas as pl
from jax.experimental.pallas import tpu as pltpu
from jax.sharding import PartitionSpec as P

BF16 = jnp.bfloat16
F32 = jnp.float32
I32 = jnp.int32
TILE = 256
EARLY = 4
ANY = pl.BlockSpec(memory_space=pl.ANY)
VMEM = pl.BlockSpec(memory_space=pltpu.VMEM)
SMEM = pl.BlockSpec(memory_space=pltpu.SMEM)
TIGHT = pltpu.CompilerParams(vmem_limit_bytes=53000 << 10)
PARAMS = pltpu.CompilerParams(vmem_limit_bytes=56 << 20)


def one_hot(columns, first, width):
    rows = columns[0].shape[0]
    wide = [jnp.broadcast_to(column, (rows, 128)).astype(jnp.int16) for column in columns]
    lane = lax.broadcasted_iota(I32, (rows, 128), 1).astype(jnp.int16)
    one = jnp.ones((rows, 128), BF16)
    zero = jnp.zeros((rows, 128), BF16)
    parts = []
    for k in range(width // 128):
        here = lane + jnp.int16(first + 128 * k)
        hit = wide[0] == here
        for other in wide[1:]:
            hit = hit | (other == here)
        parts.append(jnp.where(hit, one, zero))
    return parts[0] if len(parts) == 1 else jnp.concatenate(parts, axis=1)


def dot(a, b):
    return jnp.dot(a, b, preferred_element_type=F32)


def cost(macs, size):
    return pl.CostEstimate(flops=2 * macs, bytes_accessed=size, transcendentals=0)


def start(src, dst, sem):
    copy = pltpu.make_async_copy(src, dst, sem)
    copy.start()
    return copy


def up_kernel(live_ref, source_ref, moments_in, up_in, fine_out, high_out, pairs_out,
              fine, up, high, pairs, wide, sems):
    count, size = fine.shape
    middles = count // 8
    get_fine = start(moments_in, fine, sems.at[0])
    get_up = start(up_in, up, sems.at[1])
    cells = pairs.shape[0]
    for low in range(0, cells, 128):
        block = source_ref[:, low : min(low + 128, cells)]
        there = block.shape[1]
        if there < 128:
            block = jnp.concatenate([block, jnp.zeros((block.shape[0], 128 - there), I32)], axis=1)
        pairs[low : low + there, :] = block.T[:there, :]
    put_pairs = start(pairs, pairs_out, sems.at[2])
    live = live_ref[0]
    get_fine.wait()
    for m in range(count // TILE):
        rows = slice(m * TILE, (m + 1) * TILE)
        row = lax.broadcasted_iota(I32, (TILE, 1), 0) + m * TILE
        kept = jnp.where(row < live, fine[rows, :].astype(F32), 0.0)
        fine[rows, :] = kept.astype(BF16)
        for h in range(2):
            wide[h, rows, :] = kept[:, 128 * h : 128 * h + 128]
    put_fine = start(fine, fine_out, sems.at[0])
    get_up.wait()

    def merge(parents):
        total = None
        for k in range(8):
            rows = pl.ds(k, parents, stride=8)
            child = jnp.concatenate([wide[0, rows, :], wide[1, rows, :]], axis=1).astype(BF16)
            term = dot(child, up[k])
            total = term if total is None else total + term
        return total.astype(BF16)

    middle = merge(middles)
    high[:middles, :] = middle
    for h in range(2):
        wide[h, :middles, :] = middle[:, 128 * h : 128 * h + 128].astype(F32)
    high[middles:, :] = merge(middles // 8)
    put_high = start(high, high_out, sems.at[1])
    for put in (put_pairs, put_fine, put_high):
        put.wait()


def up_pass(live, source, moments, up):
    count, size = moments.shape
    offsets, cells = source.shape
    upper = cells - count
    return pl.pallas_call(
        up_kernel,
        out_shape=(
            jax.ShapeDtypeStruct((count, size), BF16),
            jax.ShapeDtypeStruct((upper, size), BF16),
            jax.ShapeDtypeStruct((cells, offsets), I32),
        ),
        in_specs=[SMEM, VMEM, ANY, ANY],
        out_specs=(ANY, ANY, ANY),
        scratch_shapes=[
            pltpu.VMEM((count, size), BF16),
            pltpu.VMEM(up.shape, BF16),
            pltpu.VMEM((upper, size), BF16),
            pltpu.VMEM((cells, offsets), I32),
            pltpu.VMEM((2, count, 128), F32),
            pltpu.SemaphoreType.DMA((3,)),
        ],
        compiler_params=PARAMS,
        cost_estimate=cost(count * size * size, 3 << 20),
        name="up_pass",
    )(live, source, moments, up)


def own_kernel(first, low, offsets, asked_ref, *refs):
    if first:
        fine_in, high_in, pairs_in, ops_in, picked_out, total_out = refs[:6]
        refs = refs[6:]
    else:
        fine_in, high_in, pairs_in, ops_in, total_in, picked_out, total_out = refs[:7]
        refs = refs[7:]
    table, pairs, ops, total, moved, wide, picked, sems = refs
    count = total.shape[0]
    upper = high_in.shape[0]
    steps = len(offsets)
    gets = [
        start(fine_in, table.at[pl.ds(0, count)], sems.at[0]),
        start(high_in, table.at[pl.ds(count, upper)], sems.at[1]),
        start(pairs_in, pairs, sems.at[2]),
        start(ops_in.at[pl.ds(offsets[0], steps)], ops, sems.at[3]),
    ]
    if not first:
        gets.append(start(total_in, total, sems.at[4]))
    end = table.shape[0]
    table[count + upper : end, :] = jnp.zeros((end - count - upper, table.shape[1]), BF16)
    peers, unit, slots = asked_ref.shape
    wide[...] = jnp.zeros(wide.shape, I32)
    for p in range(peers):
        wide[p : p + 1, :slots] = asked_ref[p]
    asked = wide[...].T - low
    for get in gets:
        get.wait()
    span = end - low
    if slots % 16 == 0:
        hot = jnp.concatenate(
            [one_hot([asked[:slots, p : p + 1]], 0, span) for p in range(peers)], axis=0
        )
    else:
        lane = lax.broadcasted_iota(I32, (slots, span), 1)
        hot = jnp.concatenate(
            [jnp.where(asked[:slots, p : p + 1] == lane, 1.0, 0.0) for p in range(peers)], axis=0
        ).astype(BF16)
    picked[...] = dot(hot, table[low:end, :]).astype(BF16)
    puts = [start(picked, picked_out, sems.at[0])]
    for n, o in enumerate(offsets):
        moved[n % 2] = dot(table[:count, :], ops[n]).astype(BF16)
        for m in range(count // TILE):
            rows = slice(m * TILE, (m + 1) * TILE)
            part = dot(one_hot([pairs[rows, o : o + 1]], 0, count), moved[n % 2])
            if n > 0 or not first:
                part = part + total[rows, :]
            total[rows, :] = part
    puts.append(start(total, total_out, sems.at[1]))
    for put in puts:
        put.wait()


def own_pass(low, asked, fine, high, pairs, ops, offsets, total):
    count, size = fine.shape
    first = total is None
    args = (asked, fine, high, pairs, ops) + (() if first else (total,))
    steps = len(offsets)
    replies = asked.shape[0] * asked.shape[2]
    return pl.pallas_call(
        functools.partial(own_kernel, first, low, offsets),
        out_shape=(
            jax.ShapeDtypeStruct((replies, size), BF16),
            jax.ShapeDtypeStruct((count, size), F32),
        ),
        in_specs=[VMEM] + [ANY] * (len(args) - 1),
        out_specs=(ANY, ANY),
        scratch_shapes=[
            pltpu.VMEM((count + 256, size), BF16),
            pltpu.VMEM(pairs.shape, I32),
            pltpu.VMEM((steps, size, size), BF16),
            pltpu.VMEM((count, size), F32),
            pltpu.VMEM((2, count, size), BF16),
            pltpu.VMEM((128, 128), I32),
            pltpu.VMEM((replies, size), BF16),
            pltpu.SemaphoreType.DMA((5,)),
        ],
        compiler_params=PARAMS,
        cost_estimate=cost(steps * count * size * (size + count), 4 << 20),
        name="own_pass",
    )(*args)


def near_kernel(base, asked, near_in, high_in, pairs_in, ops_in, total_in, sums_out,
                near, table, pairs, ops, total, moved, picked, sems):
    fine_slots, slots = asked
    groups = near.shape[0] // slots
    mid_slots = slots - fine_slots
    count = total_in.shape[0]
    middles = count // 8
    offsets = ops.shape[0]
    near_fine = groups * fine_slots
    near_mid = groups * mid_slots
    gets = [
        start(near_in, near, sems.at[0]),
        start(ops_in, ops, sems.at[1]),
        start(pairs_in, pairs, sems.at[2]),
        start(high_in.at[pl.ds(0, middles)], table.at[pl.ds(0, middles)], sems.at[3]),
        start(total_in, total.at[pl.ds(0, count)], sems.at[4]),
    ]
    for get in gets:
        get.wait()
    fines = jnp.concatenate(
        [near[g * slots : g * slots + fine_slots, :] for g in range(groups)], axis=0
    )
    for o in range(offsets):
        moved[o * near_fine : (o + 1) * near_fine, :] = dot(fines, ops[o]).astype(BF16)
    offset = lax.broadcasted_iota(I32, (TILE, offsets), 1) * near_fine
    width = 1536
    for m in range(count // TILE):
        rows = slice(m * TILE, (m + 1) * TILE)
        slot = pairs[rows, :] - base
        place = (slot >> 5) * fine_slots + (slot & (slots - 1)) + offset
        place = jnp.where((slot >= 0) & (slot < groups * slots), place, -1)
        part = total[rows, :]
        for first in range(0, offsets * near_fine, width):
            pieces = []
            for low in range(first, first + width, 128):
                touched = range(low // near_fine, (low + 127) // near_fine + 1)
                pieces.append(one_hot([place[:, o : o + 1] for o in touched], low, 128))
            part = part + dot(jnp.concatenate(pieces, axis=1), moved[first : first + width, :])
        total[rows, :] = part
    fines_in = pl.ds(0, count)
    puts = [start(total.at[fines_in], sums_out.at[fines_in], sems.at[0])]
    table[middles : middles + near_mid, :] = jnp.concatenate(
        [near[g * slots + fine_slots : (g + 1) * slots, :] for g in range(groups)], axis=0
    )
    table[middles + near_mid :, :] = jnp.zeros((table.shape[0] - middles - near_mid, table.shape[1]), BF16)
    source = pairs[count : count + middles, :]
    slot = source - base
    place = middles + (slot >> 5) * mid_slots + (slot & (slots - 1)) - fine_slots
    place = jnp.where((slot >= 0) & (slot < groups * slots), place, -1)
    place = jnp.where(slot < 0, source - count, place)
    for o in range(offsets):
        hot = one_hot([place[:, o : o + 1]], 0, table.shape[0])
        picked[o] = dot(hot, table[...]).astype(BF16)
    field = dot(picked[0], ops[0])
    for o in range(1, offsets):
        field = field + dot(picked[o], ops[o])
    total[count:, :] = field
    mids_in = pl.ds(count, middles)
    puts.append(start(total.at[mids_in], sums_out.at[mids_in], sems.at[1]))
    for put in puts:
        put.wait()


def near_pass(base, asked, near, high, pairs, ops, total):
    count, size = total.shape
    middles = count // 8
    offsets = ops.shape[0]
    near_fine = near.shape[0] // asked[1] * asked[0]
    macs = offsets * near_fine * size * (size + count) + 3 * offsets * middles * size * size
    return pl.pallas_call(
        functools.partial(near_kernel, base, asked),
        out_shape=jax.ShapeDtypeStruct((count + middles, size), F32),
        in_specs=[ANY] * 5,
        out_specs=ANY,
        scratch_shapes=[
            pltpu.VMEM(near.shape, BF16),
            pltpu.VMEM((256, size), BF16),
            pltpu.VMEM(pairs.shape, I32),
            pltpu.VMEM(ops.shape, BF16),
            pltpu.VMEM((count + middles, size), F32),
            pltpu.VMEM((offsets * near_fine, size), BF16),
            pltpu.VMEM((offsets, middles, size), BF16),
            pltpu.SemaphoreType.DMA((5,)),
        ],
        compiler_params=PARAMS,
        cost_estimate=cost(macs, 6 << 20),
        name="near_pass",
    )(near, high, pairs, ops, total)


def far_kernel(base, live_ref, far_ref, pairs_in, ops_in, down_in, sums_in, out_out,
               pairs, ops, down, mid, total, out, picked, mid_wide, fine_wide, sems, out_sems):
    count = total.shape[0]
    middles = mid.shape[0]
    cells = pairs.shape[0]
    offsets = ops.shape[0]
    get_pairs = start(pairs_in.at[pl.ds(count, cells)], pairs, sems.at[0])
    get_ops = start(ops_in, ops, sems.at[1])
    get_mid = start(sums_in.at[pl.ds(count, middles)], mid, sems.at[2])
    get_down = start(down_in, down, sems.at[3])
    get_total = start(sums_in.at[pl.ds(0, count)], total, sems.at[4])
    get_pairs.wait()
    place = pairs[...] - base
    for o in range(offsets):
        hot = one_hot([place[:, o : o + 1]], 0, far_ref.shape[0])
        picked[o] = dot(hot, far_ref[...]).astype(BF16)
    get_ops.wait()
    field = dot(picked[0], ops[0])
    for o in range(1, offsets):
        field = field + dot(picked[o], ops[o])
    get_mid.wait()
    get_down.wait()
    coarse = field[middles:, :].astype(BF16)
    for k in range(8):
        rows = pl.ds(k, cells - middles, stride=8)
        spread = dot(coarse, down[k])
        mid_wide[0, rows, :] = spread[:, :128]
        mid_wide[1, rows, :] = spread[:, 128:]
    spread = jnp.concatenate([mid_wide[0], mid_wide[1]], axis=1)
    local = (field[:middles, :] + mid[...] + spread).astype(BF16)
    for k in range(8):
        rows = pl.ds(k, middles, stride=8)
        spread = dot(local, down[k])
        fine_wide[0, rows, :] = spread[:, :128]
        fine_wide[1, rows, :] = spread[:, 128:]
    get_total.wait()
    live = live_ref[0]
    puts = []
    for m in range(count // TILE):
        rows = slice(m * TILE, (m + 1) * TILE)
        row = lax.broadcasted_iota(I32, (TILE, 1), 0) + m * TILE
        spread = jnp.concatenate([fine_wide[0, rows, :], fine_wide[1, rows, :]], axis=1)
        out[rows, :] = jnp.where(row < live, total[rows, :] + spread, 0.0).astype(BF16)
        puts.append(start(out.at[pl.ds(m * TILE, TILE)], out_out.at[pl.ds(m * TILE, TILE)], out_sems.at[m]))
    for put in puts:
        put.wait()


def far_pass(base, live, far, pairs, ops, down, sums):
    size = sums.shape[1]
    count = sums.shape[0] // 9 * 8
    middles = count // 8
    cells = pairs.shape[0] - count
    offsets = ops.shape[0]
    macs = offsets * cells * size * (far.shape[0] + size) + count * size * size
    return pl.pallas_call(
        functools.partial(far_kernel, base),
        out_shape=jax.ShapeDtypeStruct((count, size), BF16),
        in_specs=[SMEM, VMEM] + [ANY] * 4,
        out_specs=ANY,
        scratch_shapes=[
            pltpu.VMEM((cells, pairs.shape[1]), I32),
            pltpu.VMEM(ops.shape, BF16),
            pltpu.VMEM(down.shape, BF16),
            pltpu.VMEM((middles, size), F32),
            pltpu.VMEM((count, size), F32),
            pltpu.VMEM((count, size), BF16),
            pltpu.VMEM((offsets, cells, size), BF16),
            pltpu.VMEM((2, middles, 128), F32),
            pltpu.VMEM((2, count, 128), F32),
            pltpu.SemaphoreType.DMA((5,)),
            pltpu.SemaphoreType.DMA((count // TILE,)),
        ],
        compiler_params=TIGHT,
        cost_estimate=cost(macs, 6 << 20),
        name="far_pass",
    )(live, far, pairs, ops, down, sums)


def exchange(rows, axis):
    return lax.all_to_all(rows, axis, split_axis=0, concat_axis=0, tiled=True)


def after(value, *others):
    return lax.optimization_barrier((value,) + others)[0]


def body(
    moments, live_fine, near_requests, far_requests, pair_source, child_up, child_down, offset_ops
):
    fine_count, size = moments.shape
    offsets, cells = pair_source.shape
    slots = near_requests.shape[1]
    early = tuple(range(EARLY))
    late = tuple(range(EARLY, offsets))
    near_asked = exchange(near_requests[:, None, :], "grp")
    fine, high, pairs = up_pass(live_fine, pair_source, moments, child_up)
    far_asked = exchange(after(far_requests, high)[:, None, :], "leaf")
    replies, total = own_pass(0, near_asked, fine, high, pairs, offset_ops, early, None)
    near_tiles = exchange(replies.reshape(-1, slots, size), "grp").reshape(-1, size)
    replies, total = own_pass(
        fine_count, far_asked, fine, high, pairs, offset_ops, late, total
    )
    far_tiles = exchange(replies.reshape(far_requests.shape + (size,)), "leaf").reshape(-1, size)
    sums = near_pass(
        cells, (slots * 3 // 4, slots), near_tiles, high, pairs, offset_ops, total
    )
    far_base = cells + near_tiles.shape[0]
    return far_pass(far_base, live_fine, far_tiles, pairs, offset_ops, child_down, sums)


def solution(mesh):
    axes = ("leaf", "grp")
    in_specs = (
        P(axes, None),
        P(axes),
        P(axes, None),
        P(axes, None),
        P(axes, None),
        P(),
        P(),
        P(),
    )
    return jax.shard_map(
        body, mesh=mesh, in_specs=in_specs, out_specs=P(axes, None), check_vma=False
    )
```

```python
import functools

import jax
import jax.numpy as jnp
from jax import lax
from jax.experimental import pallas as pl
from jax.experimental.pallas import tpu as pltpu
from jax.sharding import Mesh
from jax.sharding import PartitionSpec as P

BF16 = jnp.bfloat16
F32 = jnp.float32
I32 = jnp.int32
TILE = 256
EARLY = 4
ANY = pl.BlockSpec(memory_space=pl.ANY)
VMEM = pl.BlockSpec(memory_space=pltpu.VMEM)
SMEM = pl.BlockSpec(memory_space=pltpu.SMEM)
TIGHT = pltpu.CompilerParams(vmem_limit_bytes=53000 << 10)
PARAMS = pltpu.CompilerParams(vmem_limit_bytes=56 << 20)


def one_hot(columns, first, width):
    rows = columns[0].shape[0]
    wide = [jnp.broadcast_to(column, (rows, 128)).astype(jnp.int16) for column in columns]
    lane = lax.broadcasted_iota(I32, (rows, 128), 1).astype(jnp.int16)
    one = jnp.ones((rows, 128), BF16)
    zero = jnp.zeros((rows, 128), BF16)
    parts = []
    for k in range(width // 128):
        here = lane + jnp.int16(first + 128 * k)
        hit = wide[0] == here
        for other in wide[1:]:
            hit = hit | (other == here)
        parts.append(jnp.where(hit, one, zero))
    return parts[0] if len(parts) == 1 else jnp.concatenate(parts, axis=1)


def dot(a, b):
    return jnp.dot(a, b, preferred_element_type=F32)


def cost(macs, size):
    return pl.CostEstimate(flops=2 * macs, bytes_accessed=size, transcendentals=0)


def start(src, dst, sem):
    copy = pltpu.make_async_copy(src, dst, sem)
    copy.start()
    return copy


def up_kernel(live_ref, source_ref, asks_ref, moments_in, up_in, fine_out, high_out, pairs_out, asks_out,
              fine, up, high, pairs, wide, square, sems):
    count, size = fine.shape
    middles = count // 8
    get_fine = start(moments_in, fine, sems.at[0])
    get_up = start(up_in, up, sems.at[1])
    cells = pairs.shape[0]
    for low in range(0, cells, 128):
        block = source_ref[:, low : min(low + 128, cells)]
        there = block.shape[1]
        if there < 128:
            block = jnp.concatenate([block, jnp.zeros((block.shape[0], 128 - there), I32)], axis=1)
        pairs[low : low + there, :] = block.T[:there, :]
    put_pairs = start(pairs, pairs_out, sems.at[2])
    slots, leaves = asks_ref.shape
    square[...] = jnp.zeros(square.shape, I32)
    square[:slots, :leaves] = asks_ref[...]
    square[...] = square[...].T
    own = square[pl.ds(0, leaves // 2, stride=2), :]
    other = square[pl.ds(1, leaves // 2, stride=2), :]
    asks = own + pltpu.roll(other, slots, 1)
    for chip in range(leaves // 2):
        asks_out[chip] = asks[chip : chip + 1, : 2 * slots]
    live = live_ref[0]
    get_fine.wait()
    for m in range(count // TILE):
        rows = slice(m * TILE, (m + 1) * TILE)
        row = lax.broadcasted_iota(I32, (TILE, 1), 0) + m * TILE
        kept = jnp.where(row < live, fine[rows, :].astype(F32), 0.0)
        fine[rows, :] = kept.astype(BF16)
        for h in range(2):
            wide[h, rows, :] = kept[:, 128 * h : 128 * h + 128]
    put_fine = start(fine, fine_out, sems.at[0])
    get_up.wait()

    def merge(parents):
        total = None
        for k in range(8):
            rows = pl.ds(k, parents, stride=8)
            child = jnp.concatenate([wide[0, rows, :], wide[1, rows, :]], axis=1).astype(BF16)
            term = dot(child, up[k])
            total = term if total is None else total + term
        return total.astype(BF16)

    middle = merge(middles)
    high[:middles, :] = middle
    for h in range(2):
        wide[h, :middles, :] = middle[:, 128 * h : 128 * h + 128].astype(F32)
    high[middles:, :] = merge(middles // 8)
    put_high = start(high, high_out, sems.at[1])
    for put in (put_pairs, put_fine, put_high):
        put.wait()


def up_pass(live, source, asks, moments, up):
    count, size = moments.shape
    slots, leaves = asks.shape
    offsets, cells = source.shape
    upper = cells - count
    return pl.pallas_call(
        up_kernel,
        out_shape=(
            jax.ShapeDtypeStruct((count, size), BF16),
            jax.ShapeDtypeStruct((upper, size), BF16),
            jax.ShapeDtypeStruct((cells, offsets), I32),
            jax.ShapeDtypeStruct((leaves // 2, 1, 2 * slots), I32),
        ),
        in_specs=[SMEM, VMEM, VMEM, ANY, ANY],
        out_specs=(ANY, ANY, ANY, VMEM),
        scratch_shapes=[
            pltpu.VMEM((count, size), BF16),
            pltpu.VMEM(up.shape, BF16),
            pltpu.VMEM((upper, size), BF16),
            pltpu.VMEM((cells, offsets), I32),
            pltpu.VMEM((2, count, 128), F32),
            pltpu.VMEM((128, 128), I32),
            pltpu.SemaphoreType.DMA((3,)),
        ],
        compiler_params=PARAMS,
        cost_estimate=cost(count * size * size, 3 << 20),
        name="up_pass",
    )(live, source, asks, moments, up)


def own_kernel(first, offsets, asked_ref, *refs):
    if first:
        fine_in, high_in, pairs_in, ops_in, picked_out, total_out = refs[:6]
        refs = refs[6:]
    else:
        core_ref, fine_in, high_in, other_in, pairs_in, ops_in, total_in, picked_out, total_out = refs[:9]
        refs = refs[9:]
    table, pairs, ops, total, moved, wide, picked, sems = refs
    count = total.shape[0]
    middles = count // 8
    upper = high_in.shape[0]
    steps = len(offsets)
    end = table.shape[0]
    gets = [
        start(fine_in, table.at[pl.ds(0, count)], sems.at[0]),
        start(pairs_in, pairs, sems.at[1]),
        start(ops_in.at[pl.ds(offsets[0], steps)], ops, sems.at[2]),
    ]
    if first:
        gets.append(start(high_in.at[pl.ds(0, middles)], table.at[pl.ds(count, middles)], sems.at[3]))
    else:
        gets.append(start(high_in, table.at[pl.ds(count, upper)], sems.at[3]))
        gets.append(start(other_in, table.at[pl.ds(count + upper, upper)], sems.at[4]))
        gets.append(start(total_in, total, sems.at[5]))
        used = count + 2 * upper
        table[used:end, :] = jnp.zeros((end - used, table.shape[1]), BF16)
    peers, unit, slots = asked_ref.shape
    wide[...] = jnp.zeros(wide.shape, I32)
    for p in range(peers):
        wide[p : p + 1, :slots] = asked_ref[p]
    asked = wide[...].T[:slots, :]
    if first:
        low = 0
    else:
        low = count
        here = lax.broadcasted_iota(I32, asked.shape, 0) // (slots // 2) == core_ref[0]
        asked = asked - count + jnp.where(here, 0, upper)
    for get in gets:
        get.wait()
    hot = jnp.concatenate(
        [one_hot([asked[:, p : p + 1]], 0, end - low) for p in range(peers)], axis=0
    )
    picked[...] = dot(hot, table[low:end, :]).astype(BF16)
    puts = [start(picked, picked_out, sems.at[0])]
    for n, o in enumerate(offsets):
        moved[n % 2] = dot(table[:count, :], ops[n]).astype(BF16)
        for m in range(count // TILE):
            rows = slice(m * TILE, (m + 1) * TILE)
            part = dot(one_hot([pairs[rows, o : o + 1]], 0, count), moved[n % 2])
            if n > 0 or not first:
                part = part + total[rows, :]
            total[rows, :] = part
    puts.append(start(total, total_out, sems.at[1]))
    for put in puts:
        put.wait()


def own_pass(asked, fine, high, pairs, ops, offsets, others):
    count, size = fine.shape
    first = others is None
    if first:
        args = (asked, fine, high, pairs, ops)
        specs = [VMEM] + [ANY] * 4
        rows = count + count // 8
    else:
        core, other, total = others
        args = (asked, core, fine, high, other, pairs, ops, total)
        specs = [VMEM, SMEM] + [ANY] * 6
        rows = count + 384
    steps = len(offsets)
    replies = asked.shape[0] * asked.shape[2]
    return pl.pallas_call(
        functools.partial(own_kernel, first, offsets),
        out_shape=(
            jax.ShapeDtypeStruct((replies, size), BF16),
            jax.ShapeDtypeStruct((count, size), F32),
        ),
        in_specs=specs,
        out_specs=(ANY, ANY),
        scratch_shapes=[
            pltpu.VMEM((rows, size), BF16),
            pltpu.VMEM(pairs.shape, I32),
            pltpu.VMEM((steps, size, size), BF16),
            pltpu.VMEM((count, size), F32),
            pltpu.VMEM((2, count, size), BF16),
            pltpu.VMEM((128, 128), I32),
            pltpu.VMEM((replies, size), BF16),
            pltpu.SemaphoreType.DMA((6,)),
        ],
        compiler_params=PARAMS,
        cost_estimate=cost(steps * count * size * (size + count), 4 << 20),
        name="own_pass",
    )(*args)


def near_kernel(base, asked, near_in, high_in, pairs_in, ops_in, total_in, sums_out,
                near, table, pairs, ops, total, moved, picked, sems):
    fine_slots, slots = asked
    groups = near.shape[0] // slots
    mid_slots = slots - fine_slots
    count = total_in.shape[0]
    middles = count // 8
    offsets = ops.shape[0]
    near_fine = groups * fine_slots
    near_mid = groups * mid_slots
    gets = [
        start(near_in, near, sems.at[0]),
        start(ops_in, ops, sems.at[1]),
        start(pairs_in, pairs, sems.at[2]),
        start(high_in.at[pl.ds(0, middles)], table.at[pl.ds(0, middles)], sems.at[3]),
        start(total_in, total.at[pl.ds(0, count)], sems.at[4]),
    ]
    for get in gets:
        get.wait()
    fines = jnp.concatenate(
        [near[g * slots : g * slots + fine_slots, :] for g in range(groups)], axis=0
    )
    for o in range(offsets):
        moved[o * near_fine : (o + 1) * near_fine, :] = dot(fines, ops[o]).astype(BF16)
    offset = lax.broadcasted_iota(I32, (TILE, offsets), 1) * near_fine
    width = 1536
    for m in range(count // TILE):
        rows = slice(m * TILE, (m + 1) * TILE)
        slot = pairs[rows, :] - base
        place = (slot >> 5) * fine_slots + (slot & (slots - 1)) + offset
        place = jnp.where((slot >= 0) & (slot < groups * slots), place, -1)
        part = total[rows, :]
        for first in range(0, offsets * near_fine, width):
            pieces = []
            for low in range(first, first + width, 128):
                touched = range(low // near_fine, (low + 127) // near_fine + 1)
                pieces.append(one_hot([place[:, o : o + 1] for o in touched], low, 128))
            part = part + dot(jnp.concatenate(pieces, axis=1), moved[first : first + width, :])
        total[rows, :] = part
    fines_in = pl.ds(0, count)
    puts = [start(total.at[fines_in], sums_out.at[fines_in], sems.at[0])]
    table[middles : middles + near_mid, :] = jnp.concatenate(
        [near[g * slots + fine_slots : (g + 1) * slots, :] for g in range(groups)], axis=0
    )
    table[middles + near_mid :, :] = jnp.zeros((table.shape[0] - middles - near_mid, table.shape[1]), BF16)
    source = pairs[count : count + middles, :]
    slot = source - base
    place = middles + (slot >> 5) * mid_slots + (slot & (slots - 1)) - fine_slots
    place = jnp.where((slot >= 0) & (slot < groups * slots), place, -1)
    place = jnp.where(slot < 0, source - count, place)
    for o in range(offsets):
        hot = one_hot([place[:, o : o + 1]], 0, table.shape[0])
        picked[o] = dot(hot, table[...]).astype(BF16)
    field = dot(picked[0], ops[0])
    for o in range(1, offsets):
        field = field + dot(picked[o], ops[o])
    total[count:, :] = field
    mids_in = pl.ds(count, middles)
    puts.append(start(total.at[mids_in], sums_out.at[mids_in], sems.at[1]))
    for put in puts:
        put.wait()


def near_pass(base, asked, near, high, pairs, ops, total):
    count, size = total.shape
    middles = count // 8
    offsets = ops.shape[0]
    near_fine = near.shape[0] // asked[1] * asked[0]
    macs = offsets * near_fine * size * (size + count) + 3 * offsets * middles * size * size
    return pl.pallas_call(
        functools.partial(near_kernel, base, asked),
        out_shape=jax.ShapeDtypeStruct((count + middles, size), F32),
        in_specs=[ANY] * 5,
        out_specs=ANY,
        scratch_shapes=[
            pltpu.VMEM(near.shape, BF16),
            pltpu.VMEM((256, size), BF16),
            pltpu.VMEM(pairs.shape, I32),
            pltpu.VMEM(ops.shape, BF16),
            pltpu.VMEM((count + middles, size), F32),
            pltpu.VMEM((offsets * near_fine, size), BF16),
            pltpu.VMEM((offsets, middles, size), BF16),
            pltpu.SemaphoreType.DMA((5,)),
        ],
        compiler_params=PARAMS,
        cost_estimate=cost(macs, 6 << 20),
        name="near_pass",
    )(near, high, pairs, ops, total)


def far_kernel(base, live_ref, far_ref, pairs_in, ops_in, down_in, sums_in, out_out,
               pairs, ops, down, mid, total, out, picked, mid_wide, fine_wide, sems, out_sems):
    count = total.shape[0]
    middles = mid.shape[0]
    cells = pairs.shape[0]
    offsets = ops.shape[0]
    get_pairs = start(pairs_in.at[pl.ds(count, cells)], pairs, sems.at[0])
    get_ops = start(ops_in, ops, sems.at[1])
    get_mid = start(sums_in.at[pl.ds(count, middles)], mid, sems.at[2])
    get_down = start(down_in, down, sems.at[3])
    get_total = start(sums_in.at[pl.ds(0, count)], total, sems.at[4])
    get_pairs.wait()
    place = pairs[...] - base
    for o in range(offsets):
        hot = one_hot([place[:, o : o + 1]], 0, far_ref.shape[0])
        picked[o] = dot(hot, far_ref[...]).astype(BF16)
    get_ops.wait()
    field = dot(picked[0], ops[0])
    for o in range(1, offsets):
        field = field + dot(picked[o], ops[o])
    get_mid.wait()
    get_down.wait()
    coarse = field[middles:, :].astype(BF16)
    for k in range(8):
        rows = pl.ds(k, cells - middles, stride=8)
        spread = dot(coarse, down[k])
        mid_wide[0, rows, :] = spread[:, :128]
        mid_wide[1, rows, :] = spread[:, 128:]
    spread = jnp.concatenate([mid_wide[0], mid_wide[1]], axis=1)
    local = (field[:middles, :] + mid[...] + spread).astype(BF16)
    for k in range(8):
        rows = pl.ds(k, middles, stride=8)
        spread = dot(local, down[k])
        fine_wide[0, rows, :] = spread[:, :128]
        fine_wide[1, rows, :] = spread[:, 128:]
    get_total.wait()
    live = live_ref[0]
    puts = []
    for m in range(count // TILE):
        rows = slice(m * TILE, (m + 1) * TILE)
        row = lax.broadcasted_iota(I32, (TILE, 1), 0) + m * TILE
        spread = jnp.concatenate([fine_wide[0, rows, :], fine_wide[1, rows, :]], axis=1)
        out[rows, :] = jnp.where(row < live, total[rows, :] + spread, 0.0).astype(BF16)
        puts.append(start(out.at[pl.ds(m * TILE, TILE)], out_out.at[pl.ds(m * TILE, TILE)], out_sems.at[m]))
    for put in puts:
        put.wait()


def far_pass(base, live, far, pairs, ops, down, sums):
    size = sums.shape[1]
    count = sums.shape[0] // 9 * 8
    middles = count // 8
    cells = pairs.shape[0] - count
    offsets = ops.shape[0]
    macs = offsets * cells * size * (far.shape[0] + size) + count * size * size
    return pl.pallas_call(
        functools.partial(far_kernel, base),
        out_shape=jax.ShapeDtypeStruct((count, size), BF16),
        in_specs=[SMEM, VMEM] + [ANY] * 4,
        out_specs=ANY,
        scratch_shapes=[
            pltpu.VMEM((cells, pairs.shape[1]), I32),
            pltpu.VMEM(ops.shape, BF16),
            pltpu.VMEM(down.shape, BF16),
            pltpu.VMEM((middles, size), F32),
            pltpu.VMEM((count, size), F32),
            pltpu.VMEM((count, size), BF16),
            pltpu.VMEM((offsets, cells, size), BF16),
            pltpu.VMEM((2, middles, 128), F32),
            pltpu.VMEM((2, count, 128), F32),
            pltpu.SemaphoreType.DMA((5,)),
            pltpu.SemaphoreType.DMA((count // TILE,)),
        ],
        compiler_params=TIGHT,
        cost_estimate=cost(macs, 6 << 20),
        name="far_pass",
    )(live, far, pairs, ops, down, sums)


def exchange(rows, axis):
    return lax.all_to_all(rows, axis, split_axis=0, concat_axis=0, tiled=True)


def after(value, *others):
    return lax.optimization_barrier((value,) + others)[0]


def body(
    moments, live_fine, near_requests, far_requests, pair_source, child_up, child_down, offset_ops
):
    fine_count, size = moments.shape
    offsets, cells = pair_source.shape
    slots = near_requests.shape[1]
    early = tuple(range(EARLY))
    late = tuple(range(EARLY, offsets))
    near_asked = exchange(near_requests[:, None, :], "grp")
    fine, high, pairs, asks = up_pass(
        live_fine, pair_source, far_requests.T, moments, child_up
    )
    other = lax.ppermute(high, "core", [(0, 1), (1, 0)])
    far_asked = exchange(after(asks, high), "chip")
    replies, total = own_pass(near_asked, fine, high, pairs, offset_ops, early, None)
    near_tiles = exchange(replies.reshape(-1, slots, size), "grp").reshape(-1, size)
    core = lax.axis_index("core").reshape(1)
    replies, total = own_pass(
        far_asked, fine, high, pairs, offset_ops, late, (core, other, total)
    )
    far_tiles = exchange(replies.reshape(-1, 2 * far_requests.shape[1], size), "chip")
    far_tiles = far_tiles.reshape(-1, size)
    sums = near_pass(
        cells, (slots * 3 // 4, slots), near_tiles, high, pairs, offset_ops, total
    )
    far_base = cells + near_tiles.shape[0]
    return far_pass(far_base, live_fine, far_tiles, pairs, offset_ops, child_down, sums)


def solution(mesh):
    leaf, grp = mesh.devices.shape
    axes = ("chip", "core", "grp")
    split = Mesh(mesh.devices.reshape(leaf // 2, 2, grp), axes)
    in_specs = (
        P(axes, None),
        P(axes),
        P(axes, None),
        P(axes, None),
        P(axes, None),
        P(),
        P(),
        P(),
    )
    return jax.shard_map(
        body, mesh=split, in_specs=in_specs, out_specs=P(axes, None), check_vma=False
    )
```

```python
import functools

import jax
import jax.numpy as jnp
from jax import lax
from jax.experimental import pallas as pl
from jax.experimental.pallas import tpu as pltpu
from jax.sharding import Mesh
from jax.sharding import PartitionSpec as P

BF16 = jnp.bfloat16
F32 = jnp.float32
I32 = jnp.int32
TILE = 256
EARLY = 4
LAST = 14
ANY = pl.BlockSpec(memory_space=pl.ANY)
VMEM = pl.BlockSpec(memory_space=pltpu.VMEM)
SMEM = pl.BlockSpec(memory_space=pltpu.SMEM)
TIGHT = pltpu.CompilerParams(vmem_limit_bytes=51000 << 10)
PARAMS = pltpu.CompilerParams(vmem_limit_bytes=56 << 20)


def one_hot(columns, first, width):
    rows = columns[0].shape[0]
    wide = [jnp.broadcast_to(column, (rows, 128)).astype(jnp.int16) for column in columns]
    lane = lax.broadcasted_iota(I32, (rows, 128), 1).astype(jnp.int16)
    one = jnp.ones((rows, 128), BF16)
    zero = jnp.zeros((rows, 128), BF16)
    parts = []
    for k in range(width // 128):
        here = lane + jnp.int16(first + 128 * k)
        hit = wide[0] == here
        for other in wide[1:]:
            hit = hit | (other == here)
        parts.append(jnp.where(hit, one, zero))
    return parts[0] if len(parts) == 1 else jnp.concatenate(parts, axis=1)


def dot(a, b):
    return jnp.dot(a, b, preferred_element_type=F32)


def cost(macs, size):
    return pl.CostEstimate(flops=2 * macs, bytes_accessed=size, transcendentals=0)


def start(src, dst, sem):
    copy = pltpu.make_async_copy(src, dst, sem)
    copy.start()
    return copy


def up_kernel(live_ref, source_ref, asks_ref, moments_in, up_in, fine_out, high_out, pairs_out, upper_out, asks_out,
              fine, up, high, pairs, wide, square, sems):
    count, size = fine.shape
    middles = count // 8
    get_fine = start(moments_in, fine, sems.at[0])
    get_up = start(up_in, up, sems.at[1])
    cells = pairs.shape[0]
    for low in range(0, cells, 128):
        block = source_ref[:, low : min(low + 128, cells)]
        there = block.shape[1]
        if there < 128:
            block = jnp.concatenate([block, jnp.zeros((block.shape[0], 128 - there), I32)], axis=1)
        pairs[low : low + there, :] = block.T[:there, :]
    put_pairs = start(pairs, pairs_out, sems.at[2])
    upper_out[...] = pairs[count:, :]
    slots, leaves = asks_ref.shape
    square[...] = jnp.zeros(square.shape, I32)
    square[:slots, :leaves] = asks_ref[...]
    square[...] = square[...].T
    own = square[pl.ds(0, leaves // 2, stride=2), :]
    other = square[pl.ds(1, leaves // 2, stride=2), :]
    asks = own + pltpu.roll(other, slots, 1)
    for chip in range(leaves // 2):
        asks_out[chip] = asks[chip : chip + 1, : 2 * slots]
    live = live_ref[0]
    get_fine.wait()
    for m in range(count // TILE):
        rows = slice(m * TILE, (m + 1) * TILE)
        row = lax.broadcasted_iota(I32, (TILE, 1), 0) + m * TILE
        kept = jnp.where(row < live, fine[rows, :].astype(F32), 0.0)
        fine[rows, :] = kept.astype(BF16)
        for h in range(2):
            wide[h, rows, :] = kept[:, 128 * h : 128 * h + 128]
    put_fine = start(fine, fine_out, sems.at[0])
    get_up.wait()

    def merge(parents):
        total = None
        for k in range(8):
            rows = pl.ds(k, parents, stride=8)
            child = jnp.concatenate([wide[0, rows, :], wide[1, rows, :]], axis=1).astype(BF16)
            term = dot(child, up[k])
            total = term if total is None else total + term
        return total.astype(BF16)

    middle = merge(middles)
    high[:middles, :] = middle
    for h in range(2):
        wide[h, :middles, :] = middle[:, 128 * h : 128 * h + 128].astype(F32)
    high[middles:, :] = merge(middles // 8)
    put_high = start(high, high_out, sems.at[1])
    for put in (put_pairs, put_fine, put_high):
        put.wait()


def up_pass(live, source, asks, moments, up):
    count, size = moments.shape
    slots, leaves = asks.shape
    offsets, cells = source.shape
    upper = cells - count
    return pl.pallas_call(
        up_kernel,
        out_shape=(
            jax.ShapeDtypeStruct((count, size), BF16),
            jax.ShapeDtypeStruct((upper, size), BF16),
            jax.ShapeDtypeStruct((cells, offsets), I32),
            jax.ShapeDtypeStruct((upper, offsets), I32),
            jax.ShapeDtypeStruct((leaves // 2, 1, 2 * slots), I32),
        ),
        in_specs=[SMEM, VMEM, VMEM, ANY, ANY],
        out_specs=(ANY, ANY, ANY, VMEM, VMEM),
        scratch_shapes=[
            pltpu.VMEM((count, size), BF16),
            pltpu.VMEM(up.shape, BF16),
            pltpu.VMEM((upper, size), BF16),
            pltpu.VMEM((cells, offsets), I32),
            pltpu.VMEM((2, count, 128), F32),
            pltpu.VMEM((128, 128), I32),
            pltpu.SemaphoreType.DMA((3,)),
        ],
        compiler_params=PARAMS,
        cost_estimate=cost(count * size * size, 3 << 20),
        name="up_pass",
    )(live, source, asks, moments, up)


def add_own(offsets, fine, pairs, ops, low, moved, total, fresh):
    count = fine.shape[0]
    for n, o in enumerate(offsets):
        moved[n % 2] = dot(fine[...], ops[o - low]).astype(BF16)
        for m in range(count // TILE):
            rows = slice(m * TILE, (m + 1) * TILE)
            part = dot(one_hot([pairs[rows, o : o + 1]], 0, count), moved[n % 2])
            if n > 0 or not fresh:
                part = part + total[rows, :]
            total[rows, :] = part


def own_kernel(first, offsets, asked_ref, *refs):
    if first:
        fine_in, high_in, pairs_in, ops_in, picked_out, total_out = refs[:6]
        refs = refs[6:]
    else:
        core_ref, fine_in, high_in, other_in, pairs_in, ops_in, total_in, picked_out, total_out = refs[:9]
        refs = refs[9:]
    table, pairs, ops, total, moved, wide, picked, sems = refs
    count = total.shape[0]
    middles = count // 8
    upper = high_in.shape[0]
    steps = len(offsets)
    end = table.shape[0]
    gets = [
        start(fine_in, table.at[pl.ds(0, count)], sems.at[0]),
        start(pairs_in, pairs, sems.at[1]),
        start(ops_in.at[pl.ds(offsets[0], steps)], ops, sems.at[2]),
    ]
    if first:
        gets.append(start(high_in.at[pl.ds(0, middles)], table.at[pl.ds(count, middles)], sems.at[3]))
    else:
        gets.append(start(high_in, table.at[pl.ds(count, upper)], sems.at[3]))
        gets.append(start(other_in, table.at[pl.ds(count + upper, upper)], sems.at[4]))
        gets.append(start(total_in, total, sems.at[5]))
        used = count + 2 * upper
        table[used:end, :] = jnp.zeros((end - used, table.shape[1]), BF16)
    peers, unit, slots = asked_ref.shape
    wide[...] = jnp.zeros(wide.shape, I32)
    for p in range(peers):
        wide[p : p + 1, :slots] = asked_ref[p]
    asked = wide[...].T[:slots, :]
    if first:
        low = 0
    else:
        low = count
        here = lax.broadcasted_iota(I32, asked.shape, 0) // (slots // 2) == core_ref[0]
        asked = asked - count + jnp.where(here, 0, upper)
    for get in gets:
        get.wait()
    hot = jnp.concatenate(
        [one_hot([asked[:, p : p + 1]], 0, end - low) for p in range(peers)], axis=0
    )
    picked[...] = dot(hot, table[low:end, :]).astype(BF16)
    puts = [start(picked, picked_out, sems.at[0])]
    fine = table.at[pl.ds(0, count)]
    add_own(offsets, fine, pairs, ops, offsets[0], moved, total, first)
    puts.append(start(total, total_out, sems.at[1]))
    for put in puts:
        put.wait()


def own_pass(asked, fine, high, pairs, ops, offsets, others):
    count, size = fine.shape
    first = others is None
    if first:
        args = (asked, fine, high, pairs, ops)
        specs = [VMEM] + [ANY] * 4
        rows = count + count // 8
    else:
        core, other, total = others
        args = (asked, core, fine, high, other, pairs, ops, total)
        specs = [VMEM, SMEM] + [ANY] * 6
        rows = count + 384
    steps = len(offsets)
    replies = asked.shape[0] * asked.shape[2]
    return pl.pallas_call(
        functools.partial(own_kernel, first, offsets),
        out_shape=(
            jax.ShapeDtypeStruct((replies, size), BF16),
            jax.ShapeDtypeStruct((count, size), F32),
        ),
        in_specs=specs,
        out_specs=(ANY, ANY),
        scratch_shapes=[
            pltpu.VMEM((rows, size), BF16),
            pltpu.VMEM(pairs.shape, I32),
            pltpu.VMEM((steps, size, size), BF16),
            pltpu.VMEM((count, size), F32),
            pltpu.VMEM((2, count, size), BF16),
            pltpu.VMEM((128, 128), I32),
            pltpu.VMEM((replies, size), BF16),
            pltpu.SemaphoreType.DMA((6,)),
        ],
        compiler_params=PARAMS,
        cost_estimate=cost(steps * count * size * (size + count), 4 << 20),
        name="own_pass",
    )(*args)


def near_kernel(base, asked, own, near_in, fine_in, high_in, pairs_in, ops_in, total_in, sums_out,
                near, fine, table, pairs, ops, total, moved, own_moved, picked, sems):
    fine_slots, slots = asked
    groups = near.shape[0] // slots
    mid_slots = slots - fine_slots
    count = total_in.shape[0]
    middles = count // 8
    offsets = ops.shape[0]
    near_fine = groups * fine_slots
    near_mid = groups * mid_slots
    gets = [
        start(near_in, near, sems.at[0]),
        start(fine_in, fine, sems.at[5]),
        start(ops_in, ops, sems.at[1]),
        start(pairs_in, pairs, sems.at[2]),
        start(high_in.at[pl.ds(0, middles)], table.at[pl.ds(0, middles)], sems.at[3]),
        start(total_in, total.at[pl.ds(0, count)], sems.at[4]),
    ]
    for get in gets:
        get.wait()
    fines = jnp.concatenate(
        [near[g * slots : g * slots + fine_slots, :] for g in range(groups)], axis=0
    )
    for o in range(offsets):
        moved[o * near_fine : (o + 1) * near_fine, :] = dot(fines, ops[o]).astype(BF16)
    offset = lax.broadcasted_iota(I32, (TILE, offsets), 1) * near_fine
    width = 1536
    for m in range(count // TILE):
        rows = slice(m * TILE, (m + 1) * TILE)
        slot = pairs[rows, :] - base
        place = (slot >> 5) * fine_slots + (slot & (slots - 1)) + offset
        place = jnp.where((slot >= 0) & (slot < groups * slots), place, -1)
        part = total[rows, :]
        for first in range(0, offsets * near_fine, width):
            pieces = []
            for low in range(first, first + width, 128):
                touched = range(low // near_fine, (low + 127) // near_fine + 1)
                pieces.append(one_hot([place[:, o : o + 1] for o in touched], low, 128))
            part = part + dot(jnp.concatenate(pieces, axis=1), moved[first : first + width, :])
        total[rows, :] = part
    add_own(own, fine, pairs, ops, 0, own_moved, total, False)
    fines_in = pl.ds(0, count)
    puts = [start(total.at[fines_in], sums_out.at[fines_in], sems.at[0])]
    table[middles : middles + near_mid, :] = jnp.concatenate(
        [near[g * slots + fine_slots : (g + 1) * slots, :] for g in range(groups)], axis=0
    )
    table[middles + near_mid :, :] = jnp.zeros((table.shape[0] - middles - near_mid, table.shape[1]), BF16)
    source = pairs[count : count + middles, :]
    slot = source - base
    place = middles + (slot >> 5) * mid_slots + (slot & (slots - 1)) - fine_slots
    place = jnp.where((slot >= 0) & (slot < groups * slots), place, -1)
    place = jnp.where(slot < 0, source - count, place)
    for o in range(offsets):
        hot = one_hot([place[:, o : o + 1]], 0, table.shape[0])
        picked[o] = dot(hot, table[...]).astype(BF16)
    field = dot(picked[0], ops[0])
    for o in range(1, offsets):
        field = field + dot(picked[o], ops[o])
    total[count:, :] = field
    mids_in = pl.ds(count, middles)
    puts.append(start(total.at[mids_in], sums_out.at[mids_in], sems.at[1]))
    for put in puts:
        put.wait()


def near_pass(base, asked, own, near, fine, high, pairs, ops, total):
    count, size = total.shape
    middles = count // 8
    offsets = ops.shape[0]
    near_fine = near.shape[0] // asked[1] * asked[0]
    macs = offsets * near_fine * size * (size + count) + 3 * offsets * middles * size * size
    return pl.pallas_call(
        functools.partial(near_kernel, base, asked, own),
        out_shape=jax.ShapeDtypeStruct((8 * count, size), F32),
        in_specs=[ANY] * 6,
        out_specs=ANY,
        scratch_shapes=[
            pltpu.VMEM(near.shape, BF16),
            pltpu.VMEM((count, size), BF16),
            pltpu.VMEM((256, size), BF16),
            pltpu.VMEM(pairs.shape, I32),
            pltpu.VMEM(ops.shape, BF16),
            pltpu.VMEM((count + middles, size), F32),
            pltpu.VMEM((offsets * near_fine, size), BF16),
            pltpu.VMEM((2, count, size), BF16),
            pltpu.VMEM((offsets, middles, size), BF16),
            pltpu.SemaphoreType.DMA((6,)),
        ],
        compiler_params=PARAMS,
        cost_estimate=cost(macs, 6 << 20),
        name="near_pass",
    )(near, fine, high, pairs, ops, total)


def far_kernel(base, live_ref, far_ref, pairs, ops, down, sums_in, out_out,
               mid, total, out, picked, mid_wide, fine_wide, sems, out_sems):
    count = total.shape[0]
    middles = mid.shape[0]
    cells = pairs.shape[0]
    offsets = ops.shape[0]
    get_mid = start(sums_in.at[pl.ds(count, middles)], mid, sems.at[0])
    get_total = start(sums_in.at[pl.ds(0, count)], total, sems.at[1])
    place = pairs[...] - base
    for o in range(offsets):
        hot = one_hot([place[:, o : o + 1]], 0, far_ref.shape[0])
        picked[o] = dot(hot, far_ref[...]).astype(BF16)
    field = dot(picked[0], ops[0])
    for o in range(1, offsets):
        field = field + dot(picked[o], ops[o])
    get_mid.wait()
    coarse = field[middles:, :].astype(BF16)
    for k in range(8):
        rows = pl.ds(k, cells - middles, stride=8)
        spread = dot(coarse, down[k])
        mid_wide[0, rows, :] = spread[:, :128]
        mid_wide[1, rows, :] = spread[:, 128:]
    spread = jnp.concatenate([mid_wide[0], mid_wide[1]], axis=1)
    local = (field[:middles, :] + mid[...] + spread).astype(BF16)
    for k in range(8):
        rows = pl.ds(k, middles, stride=8)
        spread = dot(local, down[k])
        fine_wide[0, rows, :] = spread[:, :128]
        fine_wide[1, rows, :] = spread[:, 128:]
    get_total.wait()
    live = live_ref[0]
    puts = []
    for m in range(count // TILE):
        rows = slice(m * TILE, (m + 1) * TILE)
        row = lax.broadcasted_iota(I32, (TILE, 1), 0) + m * TILE
        spread = jnp.concatenate([fine_wide[0, rows, :], fine_wide[1, rows, :]], axis=1)
        out[rows, :] = jnp.where(row < live, total[rows, :] + spread, 0.0).astype(BF16)
        puts.append(start(out.at[pl.ds(m * TILE, TILE)], out_out.at[pl.ds(m * TILE, TILE)], out_sems.at[m]))
    for put in puts:
        put.wait()


def far_pass(base, live, far, pairs, ops, down, sums):
    size = sums.shape[1]
    cells = pairs.shape[0]
    middles = cells // 9 * 8
    count = middles * 8
    offsets = ops.shape[0]
    macs = offsets * cells * size * (far.shape[0] + size) + count * size * size
    return pl.pallas_call(
        functools.partial(far_kernel, base),
        out_shape=jax.ShapeDtypeStruct((count, size), BF16),
        in_specs=[SMEM] + [VMEM] * 4 + [ANY],
        out_specs=ANY,
        scratch_shapes=[
            pltpu.VMEM((middles, size), F32),
            pltpu.VMEM((count, size), F32),
            pltpu.VMEM((count, size), BF16),
            pltpu.VMEM((offsets, cells, size), BF16),
            pltpu.VMEM((2, middles, 128), F32),
            pltpu.VMEM((2, count, 128), F32),
            pltpu.SemaphoreType.DMA((2,)),
            pltpu.SemaphoreType.DMA((count // TILE,)),
        ],
        compiler_params=TIGHT,
        cost_estimate=cost(macs, 6 << 20),
        name="far_pass",
    )(live, far, pairs, ops, down, sums)


def exchange(rows, axis):
    return lax.all_to_all(rows, axis, split_axis=0, concat_axis=0, tiled=True)


def after(value, *others):
    return lax.optimization_barrier((value,) + others)[0]


def body(
    moments, live_fine, near_requests, far_requests, pair_source, child_up, child_down, offset_ops
):
    fine_count, size = moments.shape
    offsets, cells = pair_source.shape
    slots = near_requests.shape[1]
    early = tuple(range(EARLY))
    late = tuple(range(EARLY, LAST))
    last = tuple(range(LAST, offsets))
    near_asked = exchange(near_requests[:, None, :], "grp")
    fine, high, pairs, upper_pairs, asks = up_pass(
        live_fine, pair_source, far_requests.T, moments, child_up
    )
    other = lax.ppermute(high, "core", [(0, 1), (1, 0)])
    far_asked = exchange(after(asks, high), "chip")
    replies, total = own_pass(near_asked, fine, high, pairs, offset_ops, early, None)
    near_tiles = exchange(replies.reshape(-1, slots, size), "grp").reshape(-1, size)
    core = lax.axis_index("core").reshape(1)
    replies, total = own_pass(
        far_asked, fine, high, pairs, offset_ops, late, (core, other, total)
    )
    far_tiles = exchange(replies.reshape(-1, 2 * far_requests.shape[1], size), "chip")
    far_tiles = far_tiles.reshape(-1, size)
    sums = near_pass(
        cells, (slots * 3 // 4, slots), last, near_tiles, fine, high, pairs, offset_ops, total
    )
    far_base = cells + near_tiles.shape[0]
    return far_pass(far_base, live_fine, far_tiles, upper_pairs, offset_ops, child_down, sums)


def solution(mesh):
    leaf, grp = mesh.devices.shape
    axes = ("chip", "core", "grp")
    split = Mesh(mesh.devices.reshape(leaf // 2, 2, grp), axes)
    in_specs = (
        P(axes, None),
        P(axes),
        P(axes, None),
        P(axes, None),
        P(axes, None),
        P(),
        P(),
        P(),
    )
    return jax.shard_map(
        body, mesh=split, in_specs=in_specs, out_specs=P(axes, None), check_vma=False
    )
```

```python
import functools

import jax
import jax.numpy as jnp
from jax import lax
from jax.experimental import pallas as pl
from jax.experimental.pallas import tpu as pltpu
from jax.sharding import Mesh
from jax.sharding import PartitionSpec as P

BF16 = jnp.bfloat16
F32 = jnp.float32
I32 = jnp.int32
TILE = 256
EARLY = 4
LAST = 14
ANY = pl.BlockSpec(memory_space=pl.ANY)
VMEM = pl.BlockSpec(memory_space=pltpu.VMEM)
SMEM = pl.BlockSpec(memory_space=pltpu.SMEM)
TIGHT = pltpu.CompilerParams(vmem_limit_bytes=52500 << 10)
PARAMS = pltpu.CompilerParams(vmem_limit_bytes=56 << 20)


def one_hot(columns, first, width):
    rows = columns[0].shape[0]
    wide = [jnp.broadcast_to(column, (rows, 128)).astype(jnp.int16) for column in columns]
    lane = lax.broadcasted_iota(I32, (rows, 128), 1).astype(jnp.int16)
    one = jnp.ones((rows, 128), BF16)
    zero = jnp.zeros((rows, 128), BF16)
    parts = []
    for k in range(width // 128):
        here = lane + jnp.int16(first + 128 * k)
        hit = wide[0] == here
        for other in wide[1:]:
            hit = hit | (other == here)
        parts.append(jnp.where(hit, one, zero))
    return parts[0] if len(parts) == 1 else jnp.concatenate(parts, axis=1)


def dot(a, b):
    return jnp.dot(a, b, preferred_element_type=F32)


def cost(macs, size):
    return pl.CostEstimate(flops=2 * macs, bytes_accessed=size, transcendentals=0)


def start(src, dst, sem):
    copy = pltpu.make_async_copy(src, dst, sem)
    copy.start()
    return copy


def up_kernel(live_ref, source_ref, asks_ref, moments_in, up_in, fine_out, high_out, pairs_out, upper_out, asks_out,
              fine, up, high, pairs, wide, square, sems):
    count, size = fine.shape
    middles = count // 8
    get_fine = start(moments_in, fine, sems.at[0])
    get_up = start(up_in, up, sems.at[1])
    cells = pairs.shape[0]
    for low in range(0, cells, 128):
        block = source_ref[:, low : min(low + 128, cells)]
        there = block.shape[1]
        if there < 128:
            block = jnp.concatenate([block, jnp.zeros((block.shape[0], 128 - there), I32)], axis=1)
        pairs[low : low + there, :] = block.T[:there, :]
    put_pairs = start(pairs, pairs_out, sems.at[2])
    upper_out[...] = pairs[count:, :]
    slots, leaves = asks_ref.shape
    square[...] = jnp.zeros(square.shape, I32)
    square[:slots, :leaves] = asks_ref[...]
    square[...] = square[...].T
    own = square[pl.ds(0, leaves // 2, stride=2), :]
    other = square[pl.ds(1, leaves // 2, stride=2), :]
    asks = own + pltpu.roll(other, slots, 1)
    for chip in range(leaves // 2):
        asks_out[chip] = asks[chip : chip + 1, : 2 * slots]
    live = live_ref[0]
    get_fine.wait()
    for m in range(count // TILE):
        rows = slice(m * TILE, (m + 1) * TILE)
        row = lax.broadcasted_iota(I32, (TILE, 1), 0) + m * TILE
        kept = jnp.where(row < live, fine[rows, :].astype(F32), 0.0)
        fine[rows, :] = kept.astype(BF16)
        for h in range(2):
            wide[h, rows, :] = kept[:, 128 * h : 128 * h + 128]
    put_fine = start(fine, fine_out, sems.at[0])
    get_up.wait()

    def merge(parents):
        total = None
        for k in range(8):
            rows = pl.ds(k, parents, stride=8)
            child = jnp.concatenate([wide[0, rows, :], wide[1, rows, :]], axis=1).astype(BF16)
            term = dot(child, up[k])
            total = term if total is None else total + term
        return total.astype(BF16)

    middle = merge(middles)
    high[:middles, :] = middle
    for h in range(2):
        wide[h, :middles, :] = middle[:, 128 * h : 128 * h + 128].astype(F32)
    high[middles:, :] = merge(middles // 8)
    put_high = start(high, high_out, sems.at[1])
    for put in (put_pairs, put_fine, put_high):
        put.wait()


def up_pass(live, source, asks, moments, up):
    count, size = moments.shape
    slots, leaves = asks.shape
    offsets, cells = source.shape
    upper = cells - count
    return pl.pallas_call(
        up_kernel,
        out_shape=(
            jax.ShapeDtypeStruct((count, size), BF16),
            jax.ShapeDtypeStruct((upper, size), BF16),
            jax.ShapeDtypeStruct((cells, offsets), I32),
            jax.ShapeDtypeStruct((upper, offsets), I32),
            jax.ShapeDtypeStruct((leaves // 2, 1, 2 * slots), I32),
        ),
        in_specs=[SMEM, VMEM, VMEM, ANY, ANY],
        out_specs=(ANY, ANY, ANY, VMEM, VMEM),
        scratch_shapes=[
            pltpu.VMEM((count, size), BF16),
            pltpu.VMEM(up.shape, BF16),
            pltpu.VMEM((upper, size), BF16),
            pltpu.VMEM((cells, offsets), I32),
            pltpu.VMEM((2, count, 128), F32),
            pltpu.VMEM((128, 128), I32),
            pltpu.SemaphoreType.DMA((3,)),
        ],
        compiler_params=PARAMS,
        cost_estimate=cost(count * size * size, 3 << 20),
        name="up_pass",
    )(live, source, asks, moments, up)


def add_own(offsets, fine, pairs, ops, low, moved, total, fresh):
    count = fine.shape[0]
    for n, o in enumerate(offsets):
        moved[n % 2] = dot(fine[...], ops[o - low]).astype(BF16)
        for m in range(count // TILE):
            rows = slice(m * TILE, (m + 1) * TILE)
            part = dot(one_hot([pairs[rows, o : o + 1]], 0, count), moved[n % 2])
            if n > 0 or not fresh:
                part = part + total[rows, :]
            total[rows, :] = part


def own_kernel(first, offsets, asked_ref, *refs):
    if first:
        fine_in, high_in, pairs_in, ops_in, picked_out, total_out = refs[:6]
        refs = refs[6:]
    else:
        core_ref, fine_in, high_in, other_in, pairs_in, ops_in, total_in, picked_out, total_out = refs[:9]
        refs = refs[9:]
    table, pairs, ops, total, moved, wide, picked, sems = refs
    count = total.shape[0]
    middles = count // 8
    upper = high_in.shape[0]
    steps = len(offsets)
    end = table.shape[0]
    gets = [
        start(fine_in, table.at[pl.ds(0, count)], sems.at[0]),
        start(pairs_in, pairs, sems.at[1]),
        start(ops_in.at[pl.ds(offsets[0], steps)], ops, sems.at[2]),
    ]
    if first:
        gets.append(start(high_in.at[pl.ds(0, middles)], table.at[pl.ds(count, middles)], sems.at[3]))
    else:
        gets.append(start(high_in, table.at[pl.ds(count, upper)], sems.at[3]))
        gets.append(start(other_in, table.at[pl.ds(count + upper, upper)], sems.at[4]))
        gets.append(start(total_in, total, sems.at[5]))
        used = count + 2 * upper
        table[used:end, :] = jnp.zeros((end - used, table.shape[1]), BF16)
    peers, unit, slots = asked_ref.shape
    wide[...] = jnp.zeros(wide.shape, I32)
    for p in range(peers):
        wide[p : p + 1, :slots] = asked_ref[p]
    asked = wide[...].T[:slots, :]
    if first:
        low = 0
    else:
        low = count
        here = lax.broadcasted_iota(I32, asked.shape, 0) // (slots // 2) == core_ref[0]
        asked = asked - count + jnp.where(here, 0, upper)
    for get in gets:
        get.wait()
    hot = jnp.concatenate(
        [one_hot([asked[:, p : p + 1]], 0, end - low) for p in range(peers)], axis=0
    )
    picked[...] = dot(hot, table[low:end, :]).astype(BF16)
    puts = [start(picked, picked_out, sems.at[0])]
    fine = table.at[pl.ds(0, count)]
    add_own(offsets, fine, pairs, ops, offsets[0], moved, total, first)
    puts.append(start(total, total_out, sems.at[1]))
    for put in puts:
        put.wait()


def own_pass(asked, fine, high, pairs, ops, offsets, others):
    count, size = fine.shape
    first = others is None
    if first:
        args = (asked, fine, high, pairs, ops)
        specs = [VMEM] + [ANY] * 4
        rows = count + count // 8
    else:
        core, other, total = others
        args = (asked, core, fine, high, other, pairs, ops, total)
        specs = [VMEM, SMEM] + [ANY] * 6
        rows = count + 384
    steps = len(offsets)
    replies = asked.shape[0] * asked.shape[2]
    return pl.pallas_call(
        functools.partial(own_kernel, first, offsets),
        out_shape=(
            jax.ShapeDtypeStruct((replies, size), BF16),
            jax.ShapeDtypeStruct((count, size), F32),
        ),
        in_specs=specs,
        out_specs=(ANY, ANY),
        scratch_shapes=[
            pltpu.VMEM((rows, size), BF16),
            pltpu.VMEM(pairs.shape, I32),
            pltpu.VMEM((steps, size, size), BF16),
            pltpu.VMEM((count, size), F32),
            pltpu.VMEM((2, count, size), BF16),
            pltpu.VMEM((128, 128), I32),
            pltpu.VMEM((replies, size), BF16),
            pltpu.SemaphoreType.DMA((6,)),
        ],
        compiler_params=PARAMS,
        cost_estimate=cost(steps * count * size * (size + count), 4 << 20),
        name="own_pass",
    )(*args)


def near_kernel(base, asked, own, near_in, fine_in, high_in, pairs_in, ops_in, total_in, sums_out,
                near, fine, table, pairs, ops, total, moved, own_moved, picked, sems):
    fine_slots, slots = asked
    groups = near.shape[0] // slots
    mid_slots = slots - fine_slots
    count = total_in.shape[0]
    middles = count // 8
    offsets = ops.shape[0]
    near_fine = groups * fine_slots
    near_mid = groups * mid_slots
    gets = [
        start(near_in, near, sems.at[0]),
        start(fine_in, fine, sems.at[5]),
        start(ops_in, ops, sems.at[1]),
        start(pairs_in, pairs, sems.at[2]),
        start(high_in.at[pl.ds(0, middles)], table.at[pl.ds(0, middles)], sems.at[3]),
        start(total_in, total.at[pl.ds(0, count)], sems.at[4]),
    ]
    for get in gets:
        get.wait()
    fines = jnp.concatenate(
        [near[g * slots : g * slots + fine_slots, :] for g in range(groups)], axis=0
    )
    for o in range(offsets):
        moved[o * near_fine : (o + 1) * near_fine, :] = dot(fines, ops[o]).astype(BF16)
    offset = lax.broadcasted_iota(I32, (TILE, offsets), 1) * near_fine
    width = 1536
    for m in range(count // TILE):
        rows = slice(m * TILE, (m + 1) * TILE)
        slot = pairs[rows, :] - base
        place = (slot >> 5) * fine_slots + (slot & (slots - 1)) + offset
        place = jnp.where((slot >= 0) & (slot < groups * slots), place, -1)
        part = total[rows, :]
        for first in range(0, offsets * near_fine, width):
            pieces = []
            for low in range(first, first + width, 128):
                touched = range(low // near_fine, (low + 127) // near_fine + 1)
                pieces.append(one_hot([place[:, o : o + 1] for o in touched], low, 128))
            part = part + dot(jnp.concatenate(pieces, axis=1), moved[first : first + width, :])
        total[rows, :] = part
    add_own(own, fine, pairs, ops, 0, own_moved, total, False)
    fines_in = pl.ds(0, count)
    puts = [start(total.at[fines_in], sums_out.at[fines_in], sems.at[0])]
    table[middles : middles + near_mid, :] = jnp.concatenate(
        [near[g * slots + fine_slots : (g + 1) * slots, :] for g in range(groups)], axis=0
    )
    table[middles + near_mid :, :] = jnp.zeros((table.shape[0] - middles - near_mid, table.shape[1]), BF16)
    source = pairs[count : count + middles, :]
    slot = source - base
    place = middles + (slot >> 5) * mid_slots + (slot & (slots - 1)) - fine_slots
    place = jnp.where((slot >= 0) & (slot < groups * slots), place, -1)
    place = jnp.where(slot < 0, source - count, place)
    for o in range(offsets):
        hot = one_hot([place[:, o : o + 1]], 0, table.shape[0])
        picked[o] = dot(hot, table[...]).astype(BF16)
    field = dot(picked[0], ops[0])
    for o in range(1, offsets):
        field = field + dot(picked[o], ops[o])
    total[count:, :] = field
    mids_in = pl.ds(count, middles)
    puts.append(start(total.at[mids_in], sums_out.at[mids_in], sems.at[1]))
    for put in puts:
        put.wait()


def near_pass(base, asked, own, near, fine, high, pairs, ops, total):
    count, size = total.shape
    middles = count // 8
    offsets = ops.shape[0]
    near_fine = near.shape[0] // asked[1] * asked[0]
    macs = offsets * near_fine * size * (size + count) + 3 * offsets * middles * size * size
    return pl.pallas_call(
        functools.partial(near_kernel, base, asked, own),
        out_shape=jax.ShapeDtypeStruct((8 * count, size), F32),
        in_specs=[ANY] * 6,
        out_specs=ANY,
        scratch_shapes=[
            pltpu.VMEM(near.shape, BF16),
            pltpu.VMEM((count, size), BF16),
            pltpu.VMEM((256, size), BF16),
            pltpu.VMEM(pairs.shape, I32),
            pltpu.VMEM(ops.shape, BF16),
            pltpu.VMEM((count + middles, size), F32),
            pltpu.VMEM((offsets * near_fine, size), BF16),
            pltpu.VMEM((2, count, size), BF16),
            pltpu.VMEM((offsets, middles, size), BF16),
            pltpu.SemaphoreType.DMA((6,)),
        ],
        compiler_params=PARAMS,
        cost_estimate=cost(macs, 6 << 20),
        name="near_pass",
    )(near, fine, high, pairs, ops, total)


def far_kernel(base, live_ref, far_ref, pairs, down, ops_in, sums_in, out_out,
               ops, mid, total, out, picked, mid_wide, fine_wide, sems, op_sems, out_sems):
    count = total.shape[0]
    middles = mid.shape[0]
    cells = pairs.shape[0]
    offsets = ops.shape[0]
    get_ops = [start(ops_in.at[o], ops.at[o], op_sems.at[o]) for o in range(offsets)]
    get_mid = start(sums_in.at[pl.ds(count, middles)], mid, sems.at[0])
    get_total = start(sums_in.at[pl.ds(0, count)], total, sems.at[1])
    place = pairs[...] - base
    for o in range(offsets):
        hot = one_hot([place[:, o : o + 1]], 0, far_ref.shape[0])
        picked[o] = dot(hot, far_ref[...]).astype(BF16)
    field = None
    for o in range(offsets):
        if o % 4 == 0:
            for get in get_ops[o : o + 4]:
                get.wait()
        term = dot(picked[o], ops[o])
        field = term if field is None else field + term
    get_mid.wait()
    coarse = field[middles:, :].astype(BF16)
    for k in range(8):
        rows = pl.ds(k, cells - middles, stride=8)
        spread = dot(coarse, down[k])
        mid_wide[0, rows, :] = spread[:, :128]
        mid_wide[1, rows, :] = spread[:, 128:]
    spread = jnp.concatenate([mid_wide[0], mid_wide[1]], axis=1)
    local = (field[:middles, :] + mid[...] + spread).astype(BF16)
    for k in range(8):
        rows = pl.ds(k, middles, stride=8)
        spread = dot(local, down[k])
        fine_wide[0, rows, :] = spread[:, :128]
        fine_wide[1, rows, :] = spread[:, 128:]
    get_total.wait()
    live = live_ref[0]
    puts = []
    for m in range(count // TILE):
        rows = slice(m * TILE, (m + 1) * TILE)
        row = lax.broadcasted_iota(I32, (TILE, 1), 0) + m * TILE
        spread = jnp.concatenate([fine_wide[0, rows, :], fine_wide[1, rows, :]], axis=1)
        out[rows, :] = jnp.where(row < live, total[rows, :] + spread, 0.0).astype(BF16)
        puts.append(start(out.at[pl.ds(m * TILE, TILE)], out_out.at[pl.ds(m * TILE, TILE)], out_sems.at[m]))
    for put in puts:
        put.wait()


def far_pass(base, live, far, pairs, ops, down, sums):
    size = sums.shape[1]
    cells = pairs.shape[0]
    middles = cells // 9 * 8
    count = middles * 8
    offsets = ops.shape[0]
    macs = offsets * cells * size * (far.shape[0] + size) + count * size * size
    return pl.pallas_call(
        functools.partial(far_kernel, base),
        out_shape=jax.ShapeDtypeStruct((count, size), BF16),
        in_specs=[SMEM] + [VMEM] * 3 + [ANY] * 2,
        out_specs=ANY,
        scratch_shapes=[
            pltpu.VMEM(ops.shape, BF16),
            pltpu.VMEM((middles, size), F32),
            pltpu.VMEM((count, size), F32),
            pltpu.VMEM((count, size), BF16),
            pltpu.VMEM((offsets, cells, size), BF16),
            pltpu.VMEM((2, middles, 128), F32),
            pltpu.VMEM((2, count, 128), F32),
            pltpu.SemaphoreType.DMA((2,)),
            pltpu.SemaphoreType.DMA((offsets,)),
            pltpu.SemaphoreType.DMA((count // TILE,)),
        ],
        compiler_params=TIGHT,
        cost_estimate=cost(macs, 6 << 20),
        name="far_pass",
    )(live, far, pairs, down, ops, sums)


def exchange(rows, axis):
    return lax.all_to_all(rows, axis, split_axis=0, concat_axis=0, tiled=True)


def after(value, *others):
    return lax.optimization_barrier((value,) + others)[0]


def body(
    moments, live_fine, near_requests, far_requests, pair_source, child_up, child_down, offset_ops
):
    fine_count, size = moments.shape
    offsets, cells = pair_source.shape
    slots = near_requests.shape[1]
    early = tuple(range(EARLY))
    late = tuple(range(EARLY, LAST))
    last = tuple(range(LAST, offsets))
    near_asked = exchange(near_requests[:, None, :], "grp")
    fine, high, pairs, upper_pairs, asks = up_pass(
        live_fine, pair_source, far_requests.T, moments, child_up
    )
    other = lax.ppermute(high, "core", [(0, 1), (1, 0)])
    far_asked = exchange(after(asks, high), "chip")
    replies, total = own_pass(near_asked, fine, high, pairs, offset_ops, early, None)
    near_tiles = exchange(replies.reshape(-1, slots, size), "grp").reshape(-1, size)
    core = lax.axis_index("core").reshape(1)
    replies, total = own_pass(
        far_asked, fine, high, pairs, offset_ops, late, (core, other, total)
    )
    far_tiles = exchange(replies.reshape(-1, 2 * far_requests.shape[1], size), "chip")
    far_tiles = far_tiles.reshape(-1, size)
    sums = near_pass(
        cells, (slots * 3 // 4, slots), last, near_tiles, fine, high, pairs, offset_ops, total
    )
    far_base = cells + near_tiles.shape[0]
    return far_pass(far_base, live_fine, far_tiles, upper_pairs, offset_ops, child_down, sums)


def solution(mesh):
    leaf, grp = mesh.devices.shape
    axes = ("chip", "core", "grp")
    split = Mesh(mesh.devices.reshape(leaf // 2, 2, grp), axes)
    in_specs = (
        P(axes, None),
        P(axes),
        P(axes, None),
        P(axes, None),
        P(axes, None),
        P(),
        P(),
        P(),
    )
    return jax.shard_map(
        body, mesh=split, in_specs=in_specs, out_specs=P(axes, None), check_vma=False
    )
```

```python
import functools

import jax
import jax.numpy as jnp
from jax import lax
from jax.experimental import pallas as pl
from jax.experimental.pallas import tpu as pltpu
from jax.sharding import Mesh
from jax.sharding import PartitionSpec as P

BF16 = jnp.bfloat16
F32 = jnp.float32
I32 = jnp.int32
TILE = 256
EARLY = 5
LAST = 15
ANY = pl.BlockSpec(memory_space=pl.ANY)
VMEM = pl.BlockSpec(memory_space=pltpu.VMEM)
SMEM = pl.BlockSpec(memory_space=pltpu.SMEM)
TIGHT = pltpu.CompilerParams(vmem_limit_bytes=51000 << 10)
PARAMS = pltpu.CompilerParams(vmem_limit_bytes=56 << 20)


def one_hot(columns, first, width):
    rows = columns[0].shape[0]
    wide = [jnp.broadcast_to(column, (rows, 128)).astype(jnp.int16) for column in columns]
    lane = lax.broadcasted_iota(I32, (rows, 128), 1).astype(jnp.int16)
    one = jnp.ones((rows, 128), BF16)
    zero = jnp.zeros((rows, 128), BF16)
    parts = []
    for k in range(width // 128):
        here = lane + jnp.int16(first + 128 * k)
        hit = wide[0] == here
        for other in wide[1:]:
            hit = hit | (other == here)
        parts.append(jnp.where(hit, one, zero))
    return parts[0] if len(parts) == 1 else jnp.concatenate(parts, axis=1)


def dot(a, b):
    return jnp.dot(a, b, preferred_element_type=F32)


def cost(macs, size):
    return pl.CostEstimate(flops=2 * macs, bytes_accessed=size, transcendentals=0)


def start(src, dst, sem):
    copy = pltpu.make_async_copy(src, dst, sem)
    copy.start()
    return copy


def up_kernel(live_ref, source_ref, asks_ref, moments_in, up_in, fine_out, high_out, pairs_out, upper_out, asks_out,
              fine, up, high, pairs, wide, square, sems):
    count, size = fine.shape
    middles = count // 8
    get_fine = start(moments_in, fine, sems.at[0])
    get_up = start(up_in, up, sems.at[1])
    cells = pairs.shape[0]
    for low in range(0, cells, 128):
        block = source_ref[:, low : min(low + 128, cells)]
        there = block.shape[1]
        if there < 128:
            block = jnp.concatenate([block, jnp.zeros((block.shape[0], 128 - there), I32)], axis=1)
        pairs[low : low + there, :] = block.T[:there, :]
    put_pairs = start(pairs, pairs_out, sems.at[2])
    upper_out[...] = pairs[count:, :]
    slots, leaves = asks_ref.shape
    square[...] = jnp.zeros(square.shape, I32)
    square[:slots, :leaves] = asks_ref[...]
    square[...] = square[...].T
    own = square[pl.ds(0, leaves // 2, stride=2), :]
    other = square[pl.ds(1, leaves // 2, stride=2), :]
    asks = own + pltpu.roll(other, slots, 1)
    for chip in range(leaves // 2):
        asks_out[chip] = asks[chip : chip + 1, : 2 * slots]
    live = live_ref[0]
    get_fine.wait()
    for m in range(count // TILE):
        rows = slice(m * TILE, (m + 1) * TILE)
        row = lax.broadcasted_iota(I32, (TILE, 1), 0) + m * TILE
        kept = jnp.where(row < live, fine[rows, :].astype(F32), 0.0)
        fine[rows, :] = kept.astype(BF16)
        for h in range(2):
            wide[h, rows, :] = kept[:, 128 * h : 128 * h + 128]
    put_fine = start(fine, fine_out, sems.at[0])
    get_up.wait()

    def merge(parents):
        total = None
        for k in range(8):
            rows = pl.ds(k, parents, stride=8)
            child = jnp.concatenate([wide[0, rows, :], wide[1, rows, :]], axis=1).astype(BF16)
            term = dot(child, up[k])
            total = term if total is None else total + term
        return total.astype(BF16)

    middle = merge(middles)
    high[:middles, :] = middle
    for h in range(2):
        wide[h, :middles, :] = middle[:, 128 * h : 128 * h + 128].astype(F32)
    high[middles:, :] = merge(middles // 8)
    put_high = start(high, high_out, sems.at[1])
    for put in (put_pairs, put_fine, put_high):
        put.wait()


def up_pass(live, source, asks, moments, up):
    count, size = moments.shape
    slots, leaves = asks.shape
    offsets, cells = source.shape
    upper = cells - count
    return pl.pallas_call(
        up_kernel,
        out_shape=(
            jax.ShapeDtypeStruct((count, size), BF16),
            jax.ShapeDtypeStruct((upper, size), BF16),
            jax.ShapeDtypeStruct((cells, offsets), I32),
            jax.ShapeDtypeStruct((upper, offsets), I32),
            jax.ShapeDtypeStruct((leaves // 2, 1, 2 * slots), I32),
        ),
        in_specs=[SMEM, VMEM, VMEM, ANY, ANY],
        out_specs=(ANY, ANY, ANY, VMEM, VMEM),
        scratch_shapes=[
            pltpu.VMEM((count, size), BF16),
            pltpu.VMEM(up.shape, BF16),
            pltpu.VMEM((upper, size), BF16),
            pltpu.VMEM((cells, offsets), I32),
            pltpu.VMEM((2, count, 128), F32),
            pltpu.VMEM((128, 128), I32),
            pltpu.SemaphoreType.DMA((3,)),
        ],
        compiler_params=PARAMS,
        cost_estimate=cost(count * size * size, 3 << 20),
        name="up_pass",
    )(live, source, asks, moments, up)


def add_own(offsets, fine, pairs, ops, low, moved, total, fresh):
    count = fine.shape[0]
    for n, o in enumerate(offsets):
        moved[n % 2] = dot(fine[...], ops[o - low]).astype(BF16)
        for m in range(count // TILE):
            rows = slice(m * TILE, (m + 1) * TILE)
            part = dot(one_hot([pairs[rows, o : o + 1]], 0, count), moved[n % 2])
            if n > 0 or not fresh:
                part = part + total[rows, :]
            total[rows, :] = part


def own_kernel(first, offsets, asked_ref, *refs):
    if first:
        fine_in, high_in, pairs_in, ops_in, picked_out, total_out = refs[:6]
        refs = refs[6:]
    else:
        core_ref, fine_in, high_in, other_in, pairs_in, ops_in, total_in, picked_out, total_out = refs[:9]
        refs = refs[9:]
    table, pairs, ops, total, moved, wide, picked, sems = refs
    count = total.shape[0]
    middles = count // 8
    upper = high_in.shape[0]
    steps = len(offsets)
    end = table.shape[0]
    gets = [
        start(fine_in, table.at[pl.ds(0, count)], sems.at[0]),
        start(pairs_in, pairs, sems.at[1]),
        start(ops_in.at[pl.ds(offsets[0], steps)], ops, sems.at[2]),
    ]
    if first:
        gets.append(start(high_in.at[pl.ds(0, middles)], table.at[pl.ds(count, middles)], sems.at[3]))
    else:
        gets.append(start(high_in, table.at[pl.ds(count, upper)], sems.at[3]))
        gets.append(start(other_in, table.at[pl.ds(count + upper, upper)], sems.at[4]))
        gets.append(start(total_in, total, sems.at[5]))
        used = count + 2 * upper
        table[used:end, :] = jnp.zeros((end - used, table.shape[1]), BF16)
    peers, unit, slots = asked_ref.shape
    wide[...] = jnp.zeros(wide.shape, I32)
    for p in range(peers):
        wide[p : p + 1, :slots] = asked_ref[p]
    asked = wide[...].T[:slots, :]
    if first:
        low = 0
    else:
        low = count
        here = lax.broadcasted_iota(I32, asked.shape, 0) // (slots // 2) == core_ref[0]
        asked = asked - count + jnp.where(here, 0, upper)
    for get in gets:
        get.wait()
    hot = jnp.concatenate(
        [one_hot([asked[:, p : p + 1]], 0, end - low) for p in range(peers)], axis=0
    )
    picked[...] = dot(hot, table[low:end, :]).astype(BF16)
    puts = [start(picked, picked_out, sems.at[0])]
    fine = table.at[pl.ds(0, count)]
    add_own(offsets, fine, pairs, ops, offsets[0], moved, total, first)
    puts.append(start(total, total_out, sems.at[1]))
    for put in puts:
        put.wait()


def own_pass(asked, fine, high, pairs, ops, offsets, others):
    count, size = fine.shape
    first = others is None
    if first:
        args = (asked, fine, high, pairs, ops)
        specs = [VMEM] + [ANY] * 4
        rows = count + count // 8
    else:
        core, other, total = others
        args = (asked, core, fine, high, other, pairs, ops, total)
        specs = [VMEM, SMEM] + [ANY] * 6
        rows = count + 384
    steps = len(offsets)
    replies = asked.shape[0] * asked.shape[2]
    return pl.pallas_call(
        functools.partial(own_kernel, first, offsets),
        out_shape=(
            jax.ShapeDtypeStruct((replies, size), BF16),
            jax.ShapeDtypeStruct((count, size), F32),
        ),
        in_specs=specs,
        out_specs=(ANY, ANY),
        scratch_shapes=[
            pltpu.VMEM((rows, size), BF16),
            pltpu.VMEM(pairs.shape, I32),
            pltpu.VMEM((steps, size, size), BF16),
            pltpu.VMEM((count, size), F32),
            pltpu.VMEM((2, count, size), BF16),
            pltpu.VMEM((128, 128), I32),
            pltpu.VMEM((replies, size), BF16),
            pltpu.SemaphoreType.DMA((6,)),
        ],
        compiler_params=PARAMS,
        cost_estimate=cost(steps * count * size * (size + count), 4 << 20),
        name="own_pass",
    )(*args)


def near_kernel(base, asked, own, near_in, fine_in, high_in, pairs_in, ops_in, total_in, sums_out,
                near, fine, table, pairs, ops, total, moved, own_moved, picked, sems):
    fine_slots, slots = asked
    groups = near.shape[0] // slots
    mid_slots = slots - fine_slots
    count = total_in.shape[0]
    middles = count // 8
    offsets = ops.shape[0]
    near_fine = groups * fine_slots
    near_mid = groups * mid_slots
    gets = [
        start(near_in, near, sems.at[0]),
        start(fine_in, fine, sems.at[5]),
        start(ops_in, ops, sems.at[1]),
        start(pairs_in, pairs, sems.at[2]),
        start(high_in.at[pl.ds(0, middles)], table.at[pl.ds(0, middles)], sems.at[3]),
        start(total_in, total.at[pl.ds(0, count)], sems.at[4]),
    ]
    for get in gets:
        get.wait()
    fines = jnp.concatenate(
        [near[g * slots : g * slots + fine_slots, :] for g in range(groups)], axis=0
    )
    for o in range(offsets):
        moved[o * near_fine : (o + 1) * near_fine, :] = dot(fines, ops[o]).astype(BF16)
    offset = lax.broadcasted_iota(I32, (TILE, offsets), 1) * near_fine
    width = 1536
    for m in range(count // TILE):
        rows = slice(m * TILE, (m + 1) * TILE)
        slot = pairs[rows, :] - base
        place = (slot >> 5) * fine_slots + (slot & (slots - 1)) + offset
        place = jnp.where((slot >= 0) & (slot < groups * slots), place, -1)
        part = total[rows, :]
        for first in range(0, offsets * near_fine, width):
            pieces = []
            for low in range(first, first + width, 128):
                touched = range(low // near_fine, (low + 127) // near_fine + 1)
                pieces.append(one_hot([place[:, o : o + 1] for o in touched], low, 128))
            part = part + dot(jnp.concatenate(pieces, axis=1), moved[first : first + width, :])
        total[rows, :] = part
    add_own(own, fine, pairs, ops, 0, own_moved, total, False)
    fines_in = pl.ds(0, count)
    puts = [start(total.at[fines_in], sums_out.at[fines_in], sems.at[0])]
    table[middles : middles + near_mid, :] = jnp.concatenate(
        [near[g * slots + fine_slots : (g + 1) * slots, :] for g in range(groups)], axis=0
    )
    table[middles + near_mid :, :] = jnp.zeros((table.shape[0] - middles - near_mid, table.shape[1]), BF16)
    source = pairs[count : count + middles, :]
    slot = source - base
    place = middles + (slot >> 5) * mid_slots + (slot & (slots - 1)) - fine_slots
    place = jnp.where((slot >= 0) & (slot < groups * slots), place, -1)
    place = jnp.where(slot < 0, source - count, place)
    for o in range(offsets):
        hot = one_hot([place[:, o : o + 1]], 0, table.shape[0])
        picked[o] = dot(hot, table[...]).astype(BF16)
    field = dot(picked[0], ops[0])
    for o in range(1, offsets):
        field = field + dot(picked[o], ops[o])
    total[count:, :] = field
    mids_in = pl.ds(count, middles)
    puts.append(start(total.at[mids_in], sums_out.at[mids_in], sems.at[1]))
    for put in puts:
        put.wait()


def near_pass(base, asked, own, near, fine, high, pairs, ops, total):
    count, size = total.shape
    middles = count // 8
    offsets = ops.shape[0]
    near_fine = near.shape[0] // asked[1] * asked[0]
    macs = offsets * near_fine * size * (size + count) + 3 * offsets * middles * size * size
    return pl.pallas_call(
        functools.partial(near_kernel, base, asked, own),
        out_shape=jax.ShapeDtypeStruct((8 * count, size), F32),
        in_specs=[ANY] * 6,
        out_specs=ANY,
        scratch_shapes=[
            pltpu.VMEM(near.shape, BF16),
            pltpu.VMEM((count, size), BF16),
            pltpu.VMEM((256, size), BF16),
            pltpu.VMEM(pairs.shape, I32),
            pltpu.VMEM(ops.shape, BF16),
            pltpu.VMEM((count + middles, size), F32),
            pltpu.VMEM((offsets * near_fine, size), BF16),
            pltpu.VMEM((2, count, size), BF16),
            pltpu.VMEM((offsets, middles, size), BF16),
            pltpu.SemaphoreType.DMA((6,)),
        ],
        compiler_params=PARAMS,
        cost_estimate=cost(macs, 6 << 20),
        name="near_pass",
    )(near, fine, high, pairs, ops, total)


def far_kernel(base, live_ref, far_ref, pairs, ops, down, sums_in, out_out,
               mid, total, out, picked, mid_wide, fine_wide, sems, out_sems):
    count = total.shape[0]
    middles = mid.shape[0]
    cells = pairs.shape[0]
    offsets = ops.shape[0]
    get_mid = start(sums_in.at[pl.ds(count, middles)], mid, sems.at[0])
    get_total = start(sums_in.at[pl.ds(0, count)], total, sems.at[1])
    place = pairs[...] - base
    for o in range(offsets):
        hot = one_hot([place[:, o : o + 1]], 0, far_ref.shape[0])
        picked[o] = dot(hot, far_ref[...]).astype(BF16)
    field = dot(picked[0], ops[0])
    for o in range(1, offsets):
        field = field + dot(picked[o], ops[o])
    get_mid.wait()
    coarse = field[middles:, :].astype(BF16)
    for k in range(8):
        rows = pl.ds(k, cells - middles, stride=8)
        spread = dot(coarse, down[k])
        mid_wide[0, rows, :] = spread[:, :128]
        mid_wide[1, rows, :] = spread[:, 128:]
    spread = jnp.concatenate([mid_wide[0], mid_wide[1]], axis=1)
    local = (field[:middles, :] + mid[...] + spread).astype(BF16)
    for k in range(8):
        rows = pl.ds(k, middles, stride=8)
        spread = dot(local, down[k])
        fine_wide[0, rows, :] = spread[:, :128]
        fine_wide[1, rows, :] = spread[:, 128:]
    get_total.wait()
    live = live_ref[0]
    puts = []
    for m in range(count // TILE):
        rows = slice(m * TILE, (m + 1) * TILE)
        row = lax.broadcasted_iota(I32, (TILE, 1), 0) + m * TILE
        spread = jnp.concatenate([fine_wide[0, rows, :], fine_wide[1, rows, :]], axis=1)
        out[rows, :] = jnp.where(row < live, total[rows, :] + spread, 0.0).astype(BF16)
        puts.append(start(out.at[pl.ds(m * TILE, TILE)], out_out.at[pl.ds(m * TILE, TILE)], out_sems.at[m]))
    for put in puts:
        put.wait()


def far_pass(base, live, far, pairs, ops, down, sums):
    size = sums.shape[1]
    cells = pairs.shape[0]
    middles = cells // 9 * 8
    count = middles * 8
    offsets = ops.shape[0]
    macs = offsets * cells * size * (far.shape[0] + size) + count * size * size
    return pl.pallas_call(
        functools.partial(far_kernel, base),
        out_shape=jax.ShapeDtypeStruct((count, size), BF16),
        in_specs=[SMEM] + [VMEM] * 4 + [ANY],
        out_specs=ANY,
        scratch_shapes=[
            pltpu.VMEM((middles, size), F32),
            pltpu.VMEM((count, size), F32),
            pltpu.VMEM((count, size), BF16),
            pltpu.VMEM((offsets, cells, size), BF16),
            pltpu.VMEM((2, middles, 128), F32),
            pltpu.VMEM((2, count, 128), F32),
            pltpu.SemaphoreType.DMA((2,)),
            pltpu.SemaphoreType.DMA((count // TILE,)),
        ],
        compiler_params=TIGHT,
        cost_estimate=cost(macs, 6 << 20),
        name="far_pass",
    )(live, far, pairs, ops, down, sums)


def exchange(rows, axis):
    return lax.all_to_all(rows, axis, split_axis=0, concat_axis=0, tiled=True)


def after(value, *others):
    return lax.optimization_barrier((value,) + others)[0]


def body(
    moments, live_fine, near_requests, far_requests, pair_source, child_up, child_down, offset_ops
):
    fine_count, size = moments.shape
    offsets, cells = pair_source.shape
    slots = near_requests.shape[1]
    early = tuple(range(EARLY))
    late = tuple(range(EARLY, LAST))
    last = tuple(range(LAST, offsets))
    near_asked = exchange(near_requests[:, None, :], "grp")
    fine, high, pairs, upper_pairs, asks = up_pass(
        live_fine, pair_source, far_requests.T, moments, child_up
    )
    other = lax.ppermute(high, "core", [(0, 1), (1, 0)])
    far_asked = exchange(after(asks, high), "chip")
    replies, total = own_pass(near_asked, fine, high, pairs, offset_ops, early, None)
    near_tiles = exchange(replies.reshape(-1, slots, size), "grp").reshape(-1, size)
    core = lax.axis_index("core").reshape(1)
    replies, total = own_pass(
        far_asked, fine, high, pairs, offset_ops, late, (core, other, total)
    )
    far_tiles = exchange(replies.reshape(-1, 2 * far_requests.shape[1], size), "chip")
    far_tiles = far_tiles.reshape(-1, size)
    sums = near_pass(
        cells, (slots * 3 // 4, slots), last, near_tiles, fine, high, pairs, offset_ops, total
    )
    far_base = cells + near_tiles.shape[0]
    return far_pass(far_base, live_fine, far_tiles, upper_pairs, offset_ops, child_down, sums)


def solution(mesh):
    leaf, grp = mesh.devices.shape
    axes = ("chip", "core", "grp")
    split = Mesh(mesh.devices.reshape(leaf // 2, 2, grp), axes)
    in_specs = (
        P(axes, None),
        P(axes),
        P(axes, None),
        P(axes, None),
        P(axes, None),
        P(),
        P(),
        P(),
    )
    return jax.shard_map(
        body, mesh=split, in_specs=in_specs, out_specs=P(axes, None), check_vma=False
    )
```
